256 devices in a mesh: tm: 2 (over core), height: 32 (over z, x), tensor: 4 (over y).
Axes of the slice: x: 4, y: 4, z: 8, core: 2. Of those that a mesh axis runs over, the one named last changes fastest.
Arguments:
- queries: bfloat16 [2, 32, 1, 256, 3072], P('tm', 'height', None, None, 'tensor'), may hold values from -8 to 8
- key_rows: bfloat16 [2, 32, 1, 256, 3072], P('tm', 'height', None, None, 'tensor'), may hold values from -6 to 6
- value_rows: bfloat16 [2, 32, 1, 256, 3072], P('tm', 'height', None, None, 'tensor'), may hold values from -6 to 6
- grad_output: bfloat16 [2, 32, 1, 256, 3072], P('tm', 'height', None, 'tensor'), may hold values from -6 to 6
- out_weight: bfloat16 [3072, 3072], P('tensor'), may hold values from -0.109375 to 0.109375
- window_flags: int32 [2, 32, 1, 9], replicated, may hold values from 0 to 1, as said below
- valid_counts: int32 [2, 32, 1], replicated, may hold values from 32 to 256, as said below
Outputs:
- grad_queries: bfloat16 [2, 32, 1, 256, 3072], P('tm', 'height', None, None, 'tensor')
- grad_keys: bfloat16 [2, 32, 1, 256, 3072], P('tm', 'height', None, None, 'tensor')
- value_rows_gradient: bfloat16 [2, 32, 1, 256, 3072], P('tm', 'height', None, None, 'tensor')
The draws below stay inside these ranges and needn't reach their ends.
Inputs may be any that keep to these rules, and one draw needn't show every extreme that they name: `window_flags`: slot s stands for the tile offset (s // 3 - 1 in time, s % 3 - 1 in height); slot 4, the tile itself, is always 1; a slot whose tile lies outside the grid is 0. `valid_counts`: tokens at a position within the tile at or beyond the count are padding; some tiles are full.
All inputs are finite; a program needn't handle non-finite values.
Results may differ from the reference program's by a relative error of at most 0.012.
Values may be sent and summed in bfloat16 or wider, within the bound.
A program may use at most 128 MiB of HBM per device.

```python
import jax
import jax.numpy as jnp
from jax import lax

D = 3072
HEADS = 24
HD = 128
TILE = 256
NW = 1
NT = 2
NH = 32


def draw_queries(key, part):
    key = jax.random.fold_in(key, 11)
    array_shape = (NT, NH, NW, TILE, HEADS * HD)
    baseline = jnp.clip(jax.random.normal(key, array_shape, jnp.float32), -6.0, 6.0)
    return baseline.astype(jnp.bfloat16)


def draw_key_rows(key, part):
    key = jax.random.fold_in(key, 12)
    array_shape = (NT, NH, NW, TILE, HEADS * HD)
    baseline = jnp.clip(jax.random.normal(key, array_shape, jnp.float32), -6.0, 6.0)
    return baseline.astype(jnp.bfloat16)


def draw_window_flags(key, part):
    key = jax.random.fold_in(key, 13)
    array_shape = (NT, NH, NW, 9)
    picked = (jax.random.randint(key, array_shape, 0, 4) != 0).astype(jnp.int32)
    slot_index = lax.broadcasted_iota(jnp.int32, array_shape, 3)
    own_row = lax.broadcasted_iota(jnp.int32, array_shape, 1)
    time_index = lax.broadcasted_iota(jnp.int32, array_shape, 0) + slot_index // 3 - 1
    row_index = own_row + slot_index % 3 - 1
    inside = (time_index >= 0) & (time_index < NT) & (row_index >= 0) & (row_index < NH)
    flags = jnp.where(inside, picked, 0)
    return jnp.where(slot_index == 4, 1, flags).astype(jnp.int32)


def draw_valid_counts(key, part):
    key = jax.random.fold_in(key, 14)
    first_key, second_key = jax.random.split(key)
    array_shape = (NT, NH, NW)
    partial_count = jax.random.randint(first_key, array_shape, max(2, TILE // 8), TILE + 1)
    chooser = jax.random.randint(second_key, array_shape, 0, 2)
    counts = jnp.where(chooser == 1, TILE, partial_count)
    linear = (lax.broadcasted_iota(jnp.int32, array_shape, 0) * NH + lax.broadcasted_iota(jnp.int32, array_shape, 1)) * NW + lax.broadcasted_iota(jnp.int32, array_shape, 2)
    return jnp.where(linear == 0, TILE, counts).astype(jnp.int32)


def block_levels(own_key, shape, cuts, smallest, top_value):
    loudness = 1.0
    for position, shards_of in cuts:
        steps = jax.random.uniform(jax.random.fold_in(jax.random.fold_in(own_key, 6), position), (shards_of,), jnp.float32, smallest / len(cuts), top_value / len(cuts))
        loudness = loudness * jnp.repeat(jnp.exp(steps), shape[position] // shards_of).reshape((-1,) + (1,) * (len(shape) - 1 - position))
    return loudness


def gaussian(own_key, shape, spread, reach, shards=(), held_as=jnp.bfloat16):
    result = jax.random.normal(own_key, shape, jnp.float32) * spread
    if len(shards) > 0:
        result = block_levels(own_key, shape, shards, -0.22, 0.18) * result
    return jnp.clip(result, min=-reach, max=reach).astype(held_as)


def setup_inputs(seed: int = 0) -> dict:
    splits = jax.random.split(jax.random.key(seed), 8)
    queries = draw_queries(jax.random.fold_in(splits[7], 71), 0)
    key_rows = draw_key_rows(jax.random.fold_in(splits[7], 71), 0)
    value_rows = gaussian(splits[2], (NT, NH, NW, TILE, HEADS * HD), 1.0, 6.0, ((0, 2), (1, 32), (4, 4)))
    grad_output = gaussian(splits[3], (NT, NH, NW, TILE, D), 1.0, 6.0, ((0, 2), (1, 32), (3, 4)))
    out_weight = gaussian(splits[4], (HEADS * HD, D), (HEADS * HD) ** -0.5, 0.109375, ((0, 4),))
    window_flags = draw_window_flags(jax.random.fold_in(splits[7], 71), 0)
    valid_counts = draw_valid_counts(jax.random.fold_in(splits[7], 71), 0)
    return dict(queries=queries, key_rows=key_rows, value_rows=value_rows, grad_output=grad_output, out_weight=out_weight, window_flags=window_flags, valid_counts=valid_counts)


def reference(queries, key_rows, value_rows, grad_output, out_weight, window_flags, valid_counts):
    time_tiles, row_tiles, col_tiles, tile_length, feature_width = queries.shape
    model_width = grad_output.shape[-1]
    softmax_scale = HD ** -0.5
    grad_attn = jnp.dot(grad_output.reshape(-1, model_width), out_weight.T, preferred_element_type=jnp.float32)
    grad_attn = grad_attn.astype(jnp.bfloat16).reshape(queries.shape)
    padding = ((1, 1), (1, 1), (0, 0), (0, 0), (0, 0))
    key_padded = jnp.pad(key_rows, padding)
    value_padded = jnp.pad(value_rows, padding)
    positions = jnp.arange(tile_length, dtype=jnp.int32)
    time_shift = jnp.array([-1, -1, -1, 0, 0, 0, 1, 1, 1], dtype=jnp.int32)
    row_shift = jnp.array([-1, 0, 1, -1, 0, 1, -1, 0, 1], dtype=jnp.int32)
    block_dimensions = (3, 3, 1, tile_length, feature_width)
    tile_shape = (1, 1, 1, tile_length, feature_width)

    def visit_neighbour(loop_carried_state, linear):
        padded_key_gradient, padded_value_gradient = loop_carried_state
        time_pos = linear // (row_tiles * col_tiles)
        row_pos = (linear // col_tiles) % row_tiles
        col_pos = linear % col_tiles
        anchor = linear * 0
        start_position = (time_pos, row_pos, col_pos, anchor, anchor)
        key_heads = lax.dynamic_slice(key_padded, start_position, block_dimensions).reshape(9 * tile_length, HEADS, HD).astype(jnp.float32)
        value_heads = lax.dynamic_slice(value_padded, start_position, block_dimensions).reshape(9 * tile_length, HEADS, HD).astype(jnp.float32)
        query_heads = lax.dynamic_slice(queries, start_position, tile_shape).reshape(tile_length, HEADS, HD).astype(jnp.float32)
        grad_heads = lax.dynamic_slice(grad_attn, start_position, tile_shape).reshape(tile_length, HEADS, HD).astype(jnp.float32)
        counts = valid_counts[jnp.clip(time_pos + time_shift, 0, time_tiles - 1), jnp.clip(row_pos + row_shift, 0, row_tiles - 1), col_pos]
        flags = window_flags[time_pos, row_pos, col_pos]
        allowed = ((flags[:, None] > 0) & (positions[None, :] < counts[:, None])).reshape(9 * tile_length)
        scores = jnp.einsum("qhd,khd->hqk", query_heads, key_heads) * softmax_scale
        scores = jnp.where(allowed[None, None, :], scores, -1.0e30)
        row_max = jnp.max(scores, axis=-1, keepdims=True)
        exponents = jnp.exp(scores - row_max)
        row_total = jnp.sum(exponents, axis=-1, keepdims=True)
        softmax = exponents / row_total
        grad_probs = jnp.einsum("qhd,khd->hqk", grad_heads, value_heads)
        row_delta = jnp.sum(softmax * grad_probs, axis=-1, keepdims=True)
        grad_scores = lax.optimization_barrier((softmax * (grad_probs - row_delta)).astype(jnp.bfloat16)).astype(jnp.float32)
        probs_low = lax.optimization_barrier(softmax.astype(jnp.bfloat16)).astype(jnp.float32)
        query_gradient = jnp.einsum("hqk,khd->qhd", grad_scores, key_heads) * softmax_scale
        grad_key = (jnp.einsum("hqk,qhd->khd", grad_scores, query_heads) * softmax_scale).reshape(block_dimensions)
        value_gradient = jnp.einsum("hqk,qhd->khd", probs_low, grad_heads).reshape(block_dimensions)
        padded_key_gradient = lax.dynamic_update_slice(padded_key_gradient, lax.dynamic_slice(padded_key_gradient, start_position, block_dimensions) + grad_key, start_position)
        padded_value_gradient = lax.dynamic_update_slice(padded_value_gradient, lax.dynamic_slice(padded_value_gradient, start_position, block_dimensions) + value_gradient, start_position)
        return (padded_key_gradient, padded_value_gradient), query_gradient.astype(jnp.bfloat16).reshape(tile_length, feature_width)

    initial_state = (jnp.zeros(key_padded.shape, jnp.float32), jnp.zeros(key_padded.shape, jnp.float32))
    tile_count_total = time_tiles * row_tiles * col_tiles
    (padded_key_gradient, padded_value_gradient), full_query_gradient = lax.scan(visit_neighbour, initial_state, jnp.arange(tile_count_total, dtype=jnp.int32))
    grad_queries = full_query_gradient.reshape(queries.shape)
    grad_keys = padded_key_gradient[1:-1, 1:-1].astype(jnp.bfloat16)
    value_rows_gradient = padded_value_gradient[1:-1, 1:-1].astype(jnp.bfloat16)
    return grad_queries, grad_keys, value_rows_gradient
```

```python
import jax
import jax.numpy as jnp
from jax import lax
from jax.experimental import pallas as pl
from jax.experimental.pallas import tpu as pltpu
from jax.sharding import PartitionSpec as P

HD = 128
SCALE = HD ** (-0.5)
LOG2E = 1.4426950408889634
MASKED = -1e30
FLOOR = -1e25
MESH = pl.DeviceIdType.MESH
F32 = jnp.float32
BF16 = jnp.bfloat16
SHARD = (0, 1, 3, 2)
NT = (((1,), (1,)), ((), ()))


def dot(a, b):
    return jnp.dot(a, b, preferred_element_type=F32)


def dot_nt(a, b):
    return lax.dot_general(a, b, NT, preferred_element_type=F32)


def kernel(
    heights,
    flags,
    counts,
    q_hbm,
    k_hbm,
    v_hbm,
    g_hbm,
    w_hbm,
    dq_hbm,
    dk_hbm,
    dv_hbm,
    qown,
    down,
    gall,
    wall,
    qx,
    dx,
    kb,
    vb,
    kt,
    bias,
    sbuf,
    probs,
    dprobs,
    dscaled,
    dk_acc,
    dv_acc,
    dk_low,
    dv_low,
    dq_part,
    dq_in,
    dq_out,
    st1,
    rv1,
    m_loc,
    c_row,
    c_col,
    st2,
    rv2,
    lsem,
    osem,
    g_s,
    g_r,
    q_s,
    q_r,
    sib_s,
    sib_r,
    d_s,
    d_r,
    s1_s,
    s1_r,
    s2_s,
    s2_r,
    p_s,
    p_r,
    e_s,
    e_r,
):
    t = lax.axis_index("tm")
    h = lax.axis_index("height")
    y = lax.axis_index("tensor")
    half = k_hbm.shape[1] // 2
    heads = half // HD
    tile = k_hbm.shape[0]
    grp = tile // 2
    shard = tile // 4
    lanes = 2 * grp
    sib = (1 - t, h, y)
    up, dn, up2, dn2 = h > 0, h < heights - 1, h > 1, h < heights - 2
    mine = pl.ds(pl.multiple_of(t * half, HD), half)
    other = pl.ds(pl.multiple_of((1 - t) * half, HD), half)

    def rows_of(k):
        return pl.ds(pl.multiple_of(lax.rem(y + SHARD[k], 4) * shard, shard), shard)

    def slot_of(ref, k):
        return ref.at[k // 2, pl.ds((k % 2) * shard, shard)]

    def remote(src, dst, ssem, rsem, dev):
        return pltpu.make_async_remote_copy(
            src_ref=src, dst_ref=dst, send_sem=ssem, recv_sem=rsem, device_id=dev, device_id_type=MESH
        )

    def arrived(dst, ssem, rsem):
        remote(dst, dst, ssem, rsem, sib).wait_recv()

    def sent(src, ssem, rsem):
        remote(src, src, ssem, rsem, sib).wait_send()

    q_loads = [pltpu.make_async_copy(q_hbm.at[rows_of(k)], slot_of(qown, k), lsem.at[k]) for k in range(4)]
    g_load = pltpu.make_async_copy(g_hbm, gall.at[0], lsem.at[4])
    k_load = pltpu.make_async_copy(k_hbm.at[:, mine], kb.at[t], lsem.at[5])
    v_load = pltpu.make_async_copy(v_hbm.at[:, mine], vb.at[t], lsem.at[6])
    w_load = pltpu.make_async_copy(w_hbm, wall, lsem.at[7])
    g_load.start()
    for cp in q_loads:
        cp.start()
    k_load.start()
    v_load.start()
    w_load.start()

    barrier = pltpu.get_barrier_semaphore()

    def greet(dev):
        pl.semaphore_signal(barrier, inc=1, device_id=dev, device_id_type=MESH)

    greet(sib)
    for k in (1, 2, 3):
        greet((t, h, lax.rem(y + k, 4)))

    @pl.when(up)
    def _():
        greet((0, h - 1, y))
        greet((1, h - 1, y))

    @pl.when(dn)
    def _():
        greet((0, h + 1, y))
        greet((1, h + 1, y))

    @pl.when(up2)
    def _():
        greet((t, h - 2, y))

    @pl.when(dn2)
    def _():
        greet((t, h + 2, y))

    def absent(b):
        qx[b] = jnp.zeros(qx.shape[1:], BF16)
        dx[b] = jnp.zeros(dx.shape[1:], BF16)
        dq_in[0, b] = jnp.zeros(dq_in.shape[2:], BF16)
        dq_in[1, b] = jnp.zeros(dq_in.shape[2:], BF16)

    nothing = jnp.full((8, lanes), FLOOR, F32)
    zeros = jnp.zeros((8, lanes), F32)

    def absent_stats(i):
        rv1[i] = nothing
        rv2[0, i] = zeros
        rv2[1, i] = zeros

    @pl.when(h == 0)
    def _():
        absent(0)
        absent_stats(1)
        absent_stats(2)

    @pl.when(h == heights - 1)
    def _():
        absent(2)
        absent_stats(3)
        absent_stats(4)

    @pl.when(h <= 1)
    def _():
        absent_stats(0)

    @pl.when(h >= heights - 2)
    def _():
        absent_stats(5)

    for b in range(3):
        st1[b] = zeros
        m_loc[b] = zeros
        st2[0, b] = zeros
        st2[1, b] = zeros
    dk_acc[...] = jnp.zeros(dk_acc.shape, F32)
    dv_acc[...] = jnp.zeros(dv_acc.shape, F32)

    position = lax.broadcasted_iota(jnp.int32, (tile, grp), 0)
    for b in range(3):
        hq = h + b - 1
        inside = (hq >= 0) & (hq < heights)
        hq = jnp.clip(hq, 0, heights - 1)
        for tq in range(2):
            for tk in range(2):
                flag = flags[tq, hq, 0, 3 * (tk - tq + 1) + 2 - b]
                count = jnp.where(inside & (flag > 0), counts[tk, h, 0], 0)
                bias[b, pl.ds(tk * tile, tile), pl.ds(tq * grp, grp)] = jnp.where(
                    position < count, 0.0, MASKED
                ).astype(F32)

    pl.semaphore_wait(
        barrier,
        4
        + 2 * up.astype(jnp.int32)
        + 2 * dn.astype(jnp.int32)
        + up2.astype(jnp.int32)
        + dn2.astype(jnp.int32),
    )

    g_load.wait()
    g_sends = [
        remote(gall.at[0], gall.at[2], g_s.at[0], g_r.at[1], (t, h, lax.rem(y + 1, 4))),
        remote(gall.at[0], gall.at[1], g_s.at[1], g_r.at[0], (t, h, lax.rem(y + 3, 4))),
        remote(gall.at[0], gall.at[3], g_s.at[2], g_r.at[2], (t, h, lax.rem(y + 2, 4))),
    ]
    for cp in g_sends:
        cp.start()
    for cp in q_loads:
        cp.wait()
    sib_sends = [
        remote(k_hbm.at[:, other], kb.at[t], sib_s.at[0], sib_r.at[0], sib),
        remote(v_hbm.at[:, other], vb.at[t], sib_s.at[1], sib_r.at[1], sib),
        remote(qown.at[:, :, other], qx.at[1, :, t], sib_s.at[2], sib_r.at[2], sib),
    ]
    for cp in sib_sends:
        cp.start()

    def part(c):
        return pl.ds(c * half, half)

    def q_send(c, d):
        return remote(
            qown.at[:, :, part(c)], qx.at[2 - 2 * d, :, t], q_s.at[d, c], q_r.at[1 - d, t], (c, h - 1 + 2 * d, y)
        )

    def both(fn):
        @pl.when(up)
        def _():
            fn(0)

        @pl.when(dn)
        def _():
            fn(1)

    both(lambda d: [q_send(c, d).start() for c in range(2)])
    q_copy = pltpu.make_async_copy(qown.at[:, :, mine], qx.at[1, :, t], lsem.at[8])
    q_copy.start()

    chunk = 128
    nk = 2 * tile
    chunks = nk // chunk

    def head(n):
        return pl.ds(n * HD, HD)

    def q_block(ref, b, g, n):
        return ref[b, g, :, :, head(n)].reshape(lanes, HD)

    def score_block(b):
        for g in range(2):
            for n in range(heads):
                qv = q_block(qx, b, g, n)
                top = jnp.full((8, lanes), FLOOR, F32)
                for i in range(chunks):
                    rows = pl.ds((i % (chunks // 2)) * chunk, chunk)
                    s = dot_nt(kb[i // (chunks // 2), rows, head(n)], qv) * (SCALE * LOG2E)
                    s = s + bias[b, pl.ds(i * chunk, chunk)]
                    sbuf[pl.ds(i * chunk, chunk)] = s
                    top = jnp.maximum(top, jnp.max(s.reshape(chunk // 8, 8, lanes), axis=0))
                m = jnp.max(top, axis=0, keepdims=True)
                total = jnp.zeros((8, lanes), F32)
                for i in range(chunks):
                    e = jnp.exp2(sbuf[pl.ds(i * chunk, chunk)] - m)
                    total = total + jnp.sum(e.reshape(chunk // 8, 8, lanes), axis=0)
                    probs[b, g, n, pl.ds(i * chunk, chunk)] = e.astype(BF16)
                total = jnp.sum(total, axis=0, keepdims=True)
                r = pl.ds(4 * g + n, 1)
                m_loc[b, r] = m
                st1[b, r] = m + jnp.log2(jnp.maximum(total, 1e-37))

    k_load.wait()
    v_load.wait()
    q_copy.wait()
    arrived(kb.at[1 - t], sib_s.at[0], sib_r.at[0])
    arrived(vb.at[1 - t], sib_s.at[1], sib_r.at[1])
    arrived(qx.at[1, :, 1 - t], sib_s.at[2], sib_r.at[2])
    for n in range(heads):
        kt[n] = jnp.transpose(kb[:, :, head(n)].reshape(nk, HD))
    score_block(1)

    w_load.wait()

    def d_send(i, c, d):
        src, dst = d_ref(i)
        return remote(
            src.at[:, part(c)], dst(2 - 2 * d), d_s.at[i, d, c], d_r.at[i, 1 - d, t], (c, h - 1 + 2 * d, y)
        )

    def d_region(i):
        return (0, pl.ds(0, grp)) if i == 0 else (1, pl.ds((i - 1) * shard, shard))

    def d_ref(i):
        g, rows = d_region(i)
        return down.at[g, rows], lambda b: dx.at[b, g, t, rows]

    def d_sib(i):
        g, rows = d_region(i)
        return remote(
            down.at[g, rows, other], dx.at[1, g, t, rows], d_s.at[i, 2, 0], d_r.at[i, 2, 0], sib
        )

    def project(i):
        g, rows = d_region(i)
        src = gall[pl.ds(0, 2)].reshape(grp, gall.shape[2]) if i == 0 else gall[1 + i]
        down[g, rows] = dot_nt(src, wall[...]).astype(BF16)
        both(lambda d: [d_send(i, c, d).start() for c in range(2)])
        d_sib(i).start()
        pltpu.make_async_copy(down.at[g, rows, mine], dx.at[1, g, t, rows], lsem.at[9 + i]).start()

    def d_wait(i):
        g, rows = d_region(i)
        pltpu.make_async_copy(down.at[g, rows, mine], dx.at[1, g, t, rows], lsem.at[9 + i]).wait()
        arrived(dx.at[1, g, 1 - t, rows], d_s.at[i, 2, 0], d_r.at[i, 2, 0])
        both(
            lambda d: [
                arrived(dx.at[2 * d, g, tq, rows], d_s.at[i, d, tq], d_r.at[i, d, tq]) for tq in range(2)
            ]
        )

    arrived(gall.at[1], g_s.at[0], g_r.at[0])
    project(0)
    arrived(gall.at[2], g_s.at[1], g_r.at[1])
    project(1)

    both(lambda d: [arrived(qx.at[2 * d, :, tq], q_s.at[d, tq], q_r.at[d, tq]) for tq in range(2)])

    @pl.loop(0, 2)
    def _(j):
        score_block(2 * j)

    def exchange(own, got, ssem, rsem):
        def copies():
            return (
                (up, remote(own.at[pl.ds(0, 2)], got.at[pl.ds(3, 2)], ssem.at[0], rsem.at[1], (t, h - 1, y))),
                (dn, remote(own.at[pl.ds(1, 2)], got.at[pl.ds(1, 2)], ssem.at[1], rsem.at[0], (t, h + 1, y))),
                (up2, remote(own.at[0], got.at[5], ssem.at[2], rsem.at[3], (t, h - 2, y))),
                (dn2, remote(own.at[2], got.at[0], ssem.at[3], rsem.at[2], (t, h + 2, y))),
            )

        def go():
            for cond, cp in copies():
                pl.when(cond)(cp.start)

        def finish():
            for cond, cp in copies():
                pl.when(cond)(cp.wait_send)
            for cond, dst, i in (
                (up, got.at[pl.ds(1, 2)], 0),
                (dn, got.at[pl.ds(3, 2)], 1),
                (up2, got.at[0], 2),
                (dn2, got.at[5], 3),
            ):
                pl.when(cond)(lambda dst=dst, i=i: arrived(dst, ssem.at[i], rsem.at[i]))

        return go, finish

    go1, finish1 = exchange(st1, rv1, s1_s, s1_r)
    go1()

    arrived(gall.at[3], g_s.at[2], g_r.at[2])
    project(2)

    finish1()
    for b in range(3):
        x0, x1, x2 = st1[b], rv1[2 * b], rv1[2 * b + 1]
        top = jnp.maximum(jnp.maximum(x0, x1), x2)
        lse = top + jnp.log2(jnp.exp2(x0 - top) + jnp.exp2(x1 - top) + jnp.exp2(x2 - top))
        c = jnp.exp2(m_loc[b] - lse)
        c_row[b] = c
        c_col[b] = jnp.transpose(c)

    def delta_block(b, g):
        for n in range(heads):
            col = c_col[b, :, pl.ds(4 * g + n, 1)]
            d = (q_block(dx, b, g, n).astype(F32) * col).astype(BF16)
            dscaled[b, g, n] = d
            total = jnp.zeros((8, lanes), F32)
            for i in range(chunks):
                rows = pl.ds((i % (chunks // 2)) * chunk, chunk)
                dp = dot_nt(vb[i // (chunks // 2), rows, head(n)], d)
                krows = pl.ds(i * chunk, chunk)
                dprobs[b, g, n, krows] = dp
                x = dp * probs[b, g, n, krows].astype(F32)
                total = total + jnp.sum(x.reshape(chunk // 8, 8, lanes), axis=0)
            st2[g, b, pl.ds(n, 1)] = jnp.sum(total, axis=0, keepdims=True)

    def value_block(b, g):
        for n in range(heads):
            dv_acc[n] += dot(probs[b, g, n], dscaled[b, g, n])

    def score_grad_block(b, g):
        delta = st2[g, b] + rv2[g, 2 * b] + rv2[g, 2 * b + 1]
        for n in range(heads):
            shift = delta[n : n + 1] * c_row[b, pl.ds(4 * g + n, 1)]
            ds = (probs[b, g, n].astype(F32) * (dprobs[b, g, n] - shift)).astype(BF16)
            dqt = dot(kt[n], ds) * SCALE
            dq = jnp.transpose(dqt).astype(BF16)
            dq_part[b, g, :, :, head(n)] = dq.reshape(2, grp, HD)
            dk_acc[n] += dot(ds, q_block(qx, b, g, n))

    ex2 = [exchange(st2.at[g], rv2.at[g], s2_s.at[g], s2_r.at[g]) for g in range(2)]

    def p_send(j, g, tq):
        return remote(
            dq_part.at[2 * j, g, tq],
            dq_in.at[t, 2 - 2 * j, g],
            p_s.at[g, j, tq],
            p_r.at[g, 1 - j, t],
            (tq, h - 1 + 2 * j, y),
        )

    def p_sib(g):
        return remote(dq_part.at[1, g, 1 - t], dq_in.at[t, 1, g], p_s.at[g, 2, 0], p_r.at[g, 2, 0], sib)

    def grads(g):
        @pl.loop(0, 2)
        def _(j):
            score_grad_block(2 * j, g)
            hh = h - 1 + 2 * j

            @pl.when((hh >= 0) & (hh < heights))
            def _():
                for tq in range(2):
                    p_send(j, g, tq).start()

        score_grad_block(1, g)
        p_sib(g).start()
        dq_in[t, 1, g] = dq_part[1, g, t]

    d_wait(0)

    @pl.loop(0, 3)
    def _(b):
        delta_block(b, 0)

    ex2[0][0]()

    @pl.loop(0, 3)
    def _(b):
        value_block(b, 0)

    d_wait(1)
    d_wait(2)

    @pl.loop(0, 3)
    def _(b):
        delta_block(b, 1)

    ex2[1][0]()
    ex2[0][1]()
    grads(0)

    @pl.loop(0, 3)
    def _(b):
        value_block(b, 1)

    for n in range(heads):
        dv_low[:, :, head(n)] = dv_acc[n].astype(BF16).reshape(2, tile, HD)
    dv_sib = remote(dv_low.at[1 - t], dv_hbm.at[:, mine], e_s.at[0], e_r.at[0], sib)
    dv_sib.start()
    dv_out = pltpu.make_async_copy(dv_low.at[t], dv_hbm.at[:, mine], osem.at[0])
    dv_out.start()

    ex2[1][1]()
    grads(1)

    for n in range(heads):
        dk_low[:, :, head(n)] = (dk_acc[n] * SCALE).astype(BF16).reshape(2, tile, HD)
    dk_sib = remote(dk_low.at[1 - t], dk_hbm.at[:, mine], e_s.at[1], e_r.at[1], sib)
    dk_sib.start()
    dk_out = pltpu.make_async_copy(dk_low.at[t], dk_hbm.at[:, mine], osem.at[1])
    dk_out.start()

    for g in range(2):
        arrived(dq_in.at[1 - t, 1, g], p_s.at[g, 2, 0], p_r.at[g, 2, 0])
        both(
            lambda d, g=g: [
                arrived(dq_in.at[c, 2 * d, g], p_s.at[g, d, c], p_r.at[g, d, c]) for c in range(2)
            ]
        )
        for c in range(2):
            x = dq_in[c, 0, g].astype(F32) + dq_in[c, 1, g].astype(F32) + dq_in[c, 2, g].astype(F32)
            dq_out[g, :, part(c)] = x.astype(BF16)
        for k in (2 * g, 2 * g + 1):
            pltpu.make_async_copy(slot_of(dq_out, k), dq_hbm.at[rows_of(k)], osem.at[2 + k]).start()

    for cp in g_sends + sib_sends:
        cp.wait_send()
    both(lambda d: [q_send(c, d).wait_send() for c in range(2)])
    for i in range(3):
        both(lambda d, i=i: [d_send(i, c, d).wait_send() for c in range(2)])
        d_sib(i).wait_send()
    for g in range(2):
        both(lambda d, g=g: [p_send(d, g, tq).wait_send() for tq in range(2)])
        p_sib(g).wait_send()
    dv_sib.wait_send()
    dk_sib.wait_send()
    arrived(dv_hbm.at[:, other], e_s.at[0], e_r.at[0])
    arrived(dk_hbm.at[:, other], e_s.at[1], e_r.at[1])
    dv_out.wait()
    dk_out.wait()
    for k in range(4):
        pltpu.make_async_copy(slot_of(dq_out, k), dq_hbm.at[rows_of(k)], osem.at[2 + k]).wait()


def local(queries, key_rows, value_rows, grad_output, out_weight, window_flags, valid_counts):
    tile, width = queries.shape[3:]
    model = grad_output.shape[-1]
    half = width // 2
    heads = half // HD
    grp, shard = tile // 2, tile // 4
    lanes, nk = 2 * grp, 2 * tile
    heights = lax.axis_size("height")
    shape = jax.ShapeDtypeStruct((tile, width), BF16)
    any_spec = pl.BlockSpec(memory_space=pl.ANY)
    smem = pl.BlockSpec(memory_space=pltpu.SMEM)
    dma = pltpu.SemaphoreType.DMA
    vm = pltpu.VMEM
    outs = pl.pallas_call(
        lambda *refs: kernel(heights, *refs),
        out_shape=(shape, shape, shape),
        in_specs=[smem, smem] + [any_spec] * 5,
        out_specs=(any_spec, any_spec, any_spec),
        scratch_shapes=[
            vm((2, grp, width), BF16),
            vm((2, grp, width), BF16),
            vm((4, shard, model), BF16),
            vm((width, model), BF16),
            vm((3, 2, 2, grp, half), BF16),
            vm((3, 2, 2, grp, half), BF16),
            vm((2, tile, half), BF16),
            vm((2, tile, half), BF16),
            vm((heads, HD, nk), BF16),
            vm((3, nk, lanes), F32),
            vm((nk, lanes), F32),
            vm((3, 2, heads, nk, lanes), BF16),
            vm((3, 2, heads, nk, lanes), F32),
            vm((3, 2, heads, lanes, HD), BF16),
            vm((heads, nk, HD), F32),
            vm((heads, nk, HD), F32),
            vm((2, tile, half), BF16),
            vm((2, tile, half), BF16),
            vm((3, 2, 2, grp, half), BF16),
            vm((2, 3, 2, grp, half), BF16),
            vm((2, grp, width), BF16),
            vm((3, 8, lanes), F32),
            vm((6, 8, lanes), F32),
            vm((3, 8, lanes), F32),
            vm((3, 8, lanes), F32),
            vm((3, lanes, 8), F32),
            vm((2, 3, 8, lanes), F32),
            vm((2, 6, 8, lanes), F32),
            dma((12,)),
            dma((6,)),
            dma((3,)),
            dma((3,)),
            dma((2, 2)),
            dma((2, 2)),
            dma((3,)),
            dma((3,)),
            dma((3, 3, 2)),
            dma((3, 3, 2)),
            dma((4,)),
            dma((4,)),
            dma((2, 4)),
            dma((2, 4)),
            dma((2, 3, 2)),
            dma((2, 3, 2)),
            dma((2,)),
            dma((2,)),
        ],
        compiler_params=pltpu.CompilerParams(
            collective_id=0, has_side_effects=True, vmem_limit_bytes=56 * 2**20
        ),
    )(
        window_flags,
        valid_counts,
        queries.reshape(tile, width),
        key_rows.reshape(tile, width),
        value_rows.reshape(tile, width),
        grad_output.reshape(grad_output.shape[3], model),
        out_weight,
    )
    return tuple(x.reshape(queries.shape) for x in outs)


def solution(mesh):
    wide = P("tm", "height", None, None, "tensor")
    placed = (wide, wide, wide, P("tm", "height", None, "tensor", None), P("tensor", None), P(), P())
    return jax.shard_map(local, mesh=mesh, in_specs=placed, out_specs=(wide, wide, wide), check_vma=False)
```

```python
import jax
import jax.numpy as jnp
from jax import lax
from jax.experimental import pallas as pl
from jax.experimental.pallas import tpu as pltpu
from jax.sharding import PartitionSpec as P

HD = 128
SCALE = HD ** (-0.5)
LOG2E = 1.4426950408889634
MASKED = -1e30
FLOOR = -1e25
MESH = pl.DeviceIdType.MESH
F32 = jnp.float32
BF16 = jnp.bfloat16
SHARD = (0, 1, 3, 2)
NT = (((1,), (1,)), ((), ()))


def dot(a, b):
    return jnp.dot(a, b, preferred_element_type=F32)


def dot_nt(a, b):
    return lax.dot_general(a, b, NT, preferred_element_type=F32)


def kernel(
    heights,
    f_hbm,
    n_hbm,
    q_hbm,
    k_hbm,
    v_hbm,
    g_hbm,
    w_hbm,
    dq_hbm,
    dk_hbm,
    dv_hbm,
    flags,
    counts,
    qown,
    down,
    gall,
    wall,
    qx,
    dx,
    kb,
    vb,
    kt,
    bias,
    sbuf,
    probs,
    dprobs,
    dscaled,
    dk_acc,
    dv_acc,
    dk_low,
    dv_low,
    dq_part,
    dq_in,
    dq_out,
    st1,
    rv1,
    m_loc,
    c_row,
    c_col,
    st2,
    rv2,
    lsem,
    osem,
    g_s,
    g_r,
    q_s,
    q_r,
    sib_s,
    sib_r,
    d_s,
    d_r,
    s1_s,
    s1_r,
    s2_s,
    s2_r,
    p_s,
    p_r,
    e_s,
    e_r,
):
    t = lax.axis_index("tm")
    h = lax.axis_index("height")
    y = lax.axis_index("tensor")
    half = k_hbm.shape[1] // 2
    heads = half // HD
    tile = k_hbm.shape[0]
    grp = tile // 2
    shard = tile // 4
    lanes = 2 * grp
    sib = (1 - t, h, y)
    up, dn, up2, dn2 = h > 0, h < heights - 1, h > 1, h < heights - 2
    mine = pl.ds(pl.multiple_of(t * half, HD), half)
    other = pl.ds(pl.multiple_of((1 - t) * half, HD), half)

    def rows_of(k):
        return pl.ds(pl.multiple_of(lax.rem(y + SHARD[k], 4) * shard, shard), shard)

    def slot_of(ref, k):
        return ref.at[k // 2, pl.ds((k % 2) * shard, shard)]

    def remote(src, dst, ssem, rsem, dev):
        return pltpu.make_async_remote_copy(
            src_ref=src, dst_ref=dst, send_sem=ssem, recv_sem=rsem, device_id=dev, device_id_type=MESH
        )

    def arrived(dst, ssem, rsem):
        remote(dst, dst, ssem, rsem, sib).wait_recv()

    def sent(src, ssem, rsem):
        remote(src, src, ssem, rsem, sib).wait_send()

    q_loads = [pltpu.make_async_copy(q_hbm.at[rows_of(k)], slot_of(qown, k), lsem.at[k]) for k in range(4)]
    g_load = pltpu.make_async_copy(g_hbm, gall.at[0], lsem.at[4])
    k_load = pltpu.make_async_copy(k_hbm.at[:, mine], kb.at[t], lsem.at[5])
    v_load = pltpu.make_async_copy(v_hbm.at[:, mine], vb.at[t], lsem.at[6])
    w_load = pltpu.make_async_copy(w_hbm, wall, lsem.at[7])
    f_load = pltpu.make_async_copy(f_hbm, flags, lsem.at[12])
    n_load = pltpu.make_async_copy(n_hbm, counts, lsem.at[13])
    f_load.start()
    n_load.start()
    g_load.start()
    for cp in q_loads:
        cp.start()
    k_load.start()
    v_load.start()
    w_load.start()

    barrier = pltpu.get_barrier_semaphore()

    def greet(dev):
        pl.semaphore_signal(barrier, inc=1, device_id=dev, device_id_type=MESH)

    greet(sib)
    for k in (1, 2, 3):
        greet((t, h, lax.rem(y + k, 4)))

    @pl.when(up)
    def _():
        greet((0, h - 1, y))
        greet((1, h - 1, y))

    @pl.when(dn)
    def _():
        greet((0, h + 1, y))
        greet((1, h + 1, y))

    @pl.when(up2)
    def _():
        greet((t, h - 2, y))

    @pl.when(dn2)
    def _():
        greet((t, h + 2, y))

    def absent(b):
        qx[b] = jnp.zeros(qx.shape[1:], BF16)
        dx[b] = jnp.zeros(dx.shape[1:], BF16)
        dq_in[0, b] = jnp.zeros(dq_in.shape[2:], BF16)
        dq_in[1, b] = jnp.zeros(dq_in.shape[2:], BF16)

    nothing = jnp.full((8, lanes), FLOOR, F32)
    zeros = jnp.zeros((8, lanes), F32)

    def absent_stats(i):
        rv1[i] = nothing
        rv2[0, i] = zeros
        rv2[1, i] = zeros

    @pl.when(h == 0)
    def _():
        absent(0)
        absent_stats(1)
        absent_stats(2)

    @pl.when(h == heights - 1)
    def _():
        absent(2)
        absent_stats(3)
        absent_stats(4)

    @pl.when(h <= 1)
    def _():
        absent_stats(0)

    @pl.when(h >= heights - 2)
    def _():
        absent_stats(5)

    for b in range(3):
        st1[b] = zeros
        m_loc[b] = zeros
        st2[0, b] = zeros
        st2[1, b] = zeros
    dk_acc[...] = jnp.zeros(dk_acc.shape, F32)
    dv_acc[...] = jnp.zeros(dv_acc.shape, F32)

    f_load.wait()
    n_load.wait()
    position = lax.broadcasted_iota(jnp.int32, (tile, grp), 0).astype(F32)
    lane = lax.broadcasted_iota(jnp.int32, (1, heights), 1)

    def at_height(row, i):
        return jnp.sum(jnp.where(lane == i, row.astype(F32), 0.0), axis=1, keepdims=True)

    for b in range(3):
        hq = h + b - 1
        inside = (hq >= 0) & (hq < heights)
        hq = jnp.clip(hq, 0, heights - 1)
        for tq in range(2):
            for tk in range(2):
                flag = at_height(flags[tq, 3 * (tk - tq + 1) + 2 - b], hq)
                count = jnp.where(inside & (flag > 0.0), at_height(counts[tk], h), 0.0)
                bias[b, pl.ds(tk * tile, tile), pl.ds(tq * grp, grp)] = jnp.where(
                    position < count, 0.0, MASKED
                ).astype(F32)

    pl.semaphore_wait(
        barrier,
        4
        + 2 * up.astype(jnp.int32)
        + 2 * dn.astype(jnp.int32)
        + up2.astype(jnp.int32)
        + dn2.astype(jnp.int32),
    )

    g_load.wait()
    g_sends = [
        remote(gall.at[0], gall.at[2], g_s.at[0], g_r.at[1], (t, h, lax.rem(y + 1, 4))),
        remote(gall.at[0], gall.at[1], g_s.at[1], g_r.at[0], (t, h, lax.rem(y + 3, 4))),
        remote(gall.at[0], gall.at[3], g_s.at[2], g_r.at[2], (t, h, lax.rem(y + 2, 4))),
    ]
    for cp in g_sends:
        cp.start()
    for cp in q_loads:
        cp.wait()
    sib_sends = [
        remote(k_hbm.at[:, other], kb.at[t], sib_s.at[0], sib_r.at[0], sib),
        remote(v_hbm.at[:, other], vb.at[t], sib_s.at[1], sib_r.at[1], sib),
        remote(qown.at[:, :, other], qx.at[1, :, t], sib_s.at[2], sib_r.at[2], sib),
    ]
    for cp in sib_sends:
        cp.start()

    def part(c):
        return pl.ds(c * half, half)

    def q_send(c, d):
        return remote(
            qown.at[:, :, part(c)], qx.at[2 - 2 * d, :, t], q_s.at[d, c], q_r.at[1 - d, t], (c, h - 1 + 2 * d, y)
        )

    def both(fn):
        @pl.when(up)
        def _():
            fn(0)

        @pl.when(dn)
        def _():
            fn(1)

    both(lambda d: [q_send(c, d).start() for c in range(2)])
    q_copy = pltpu.make_async_copy(qown.at[:, :, mine], qx.at[1, :, t], lsem.at[8])
    q_copy.start()

    chunk = 128
    nk = 2 * tile
    chunks = nk // chunk

    def head(n):
        return pl.ds(n * HD, HD)

    def q_block(ref, b, g, n):
        return ref[b, g, :, :, head(n)].reshape(lanes, HD)

    def score_block(b):
        for g in range(2):
            for n in range(heads):
                qv = q_block(qx, b, g, n)
                top = jnp.full((8, lanes), FLOOR, F32)
                for i in range(chunks):
                    rows = pl.ds((i % (chunks // 2)) * chunk, chunk)
                    s = dot_nt(kb[i // (chunks // 2), rows, head(n)], qv) * (SCALE * LOG2E)
                    s = s + bias[b, pl.ds(i * chunk, chunk)]
                    sbuf[pl.ds(i * chunk, chunk)] = s
                    top = jnp.maximum(top, jnp.max(s.reshape(chunk // 8, 8, lanes), axis=0))
                m = jnp.max(top, axis=0, keepdims=True)
                total = jnp.zeros((8, lanes), F32)
                for i in range(chunks):
                    e = jnp.exp2(sbuf[pl.ds(i * chunk, chunk)] - m)
                    total = total + jnp.sum(e.reshape(chunk // 8, 8, lanes), axis=0)
                    probs[b, g, n, pl.ds(i * chunk, chunk)] = e.astype(BF16)
                total = jnp.sum(total, axis=0, keepdims=True)
                r = pl.ds(4 * g + n, 1)
                m_loc[b, r] = m
                st1[b, r] = m + jnp.log2(jnp.maximum(total, 1e-37))

    k_load.wait()
    v_load.wait()
    q_copy.wait()
    arrived(kb.at[1 - t], sib_s.at[0], sib_r.at[0])
    arrived(vb.at[1 - t], sib_s.at[1], sib_r.at[1])
    arrived(qx.at[1, :, 1 - t], sib_s.at[2], sib_r.at[2])
    for n in range(heads):
        kt[n] = jnp.transpose(kb[:, :, head(n)].reshape(nk, HD))
    score_block(1)

    w_load.wait()

    def d_send(i, c, d):
        src, dst = d_ref(i)
        return remote(
            src.at[:, part(c)], dst(2 - 2 * d), d_s.at[i, d, c], d_r.at[i, 1 - d, t], (c, h - 1 + 2 * d, y)
        )

    def d_region(i):
        return (0, pl.ds(0, grp)) if i == 0 else (1, pl.ds((i - 1) * shard, shard))

    def d_ref(i):
        g, rows = d_region(i)
        return down.at[g, rows], lambda b: dx.at[b, g, t, rows]

    def d_sib(i):
        g, rows = d_region(i)
        return remote(
            down.at[g, rows, other], dx.at[1, g, t, rows], d_s.at[i, 2, 0], d_r.at[i, 2, 0], sib
        )

    def project(i):
        g, rows = d_region(i)
        src = gall[pl.ds(0, 2)].reshape(grp, gall.shape[2]) if i == 0 else gall[1 + i]
        down[g, rows] = dot_nt(src, wall[...]).astype(BF16)
        both(lambda d: [d_send(i, c, d).start() for c in range(2)])
        d_sib(i).start()
        pltpu.make_async_copy(down.at[g, rows, mine], dx.at[1, g, t, rows], lsem.at[9 + i]).start()

    def d_wait(i):
        g, rows = d_region(i)
        pltpu.make_async_copy(down.at[g, rows, mine], dx.at[1, g, t, rows], lsem.at[9 + i]).wait()
        arrived(dx.at[1, g, 1 - t, rows], d_s.at[i, 2, 0], d_r.at[i, 2, 0])
        both(
            lambda d: [
                arrived(dx.at[2 * d, g, tq, rows], d_s.at[i, d, tq], d_r.at[i, d, tq]) for tq in range(2)
            ]
        )

    arrived(gall.at[1], g_s.at[0], g_r.at[0])
    project(0)
    arrived(gall.at[2], g_s.at[1], g_r.at[1])
    project(1)

    both(lambda d: [arrived(qx.at[2 * d, :, tq], q_s.at[d, tq], q_r.at[d, tq]) for tq in range(2)])

    @pl.loop(0, 2)
    def _(j):
        score_block(2 * j)

    def exchange(own, got, ssem, rsem):
        def copies():
            return (
                (up, remote(own.at[pl.ds(0, 2)], got.at[pl.ds(3, 2)], ssem.at[0], rsem.at[1], (t, h - 1, y))),
                (dn, remote(own.at[pl.ds(1, 2)], got.at[pl.ds(1, 2)], ssem.at[1], rsem.at[0], (t, h + 1, y))),
                (up2, remote(own.at[0], got.at[5], ssem.at[2], rsem.at[3], (t, h - 2, y))),
                (dn2, remote(own.at[2], got.at[0], ssem.at[3], rsem.at[2], (t, h + 2, y))),
            )

        def go():
            for cond, cp in copies():
                pl.when(cond)(cp.start)

        def finish():
            for cond, cp in copies():
                pl.when(cond)(cp.wait_send)
            for cond, dst, i in (
                (up, got.at[pl.ds(1, 2)], 0),
                (dn, got.at[pl.ds(3, 2)], 1),
                (up2, got.at[0], 2),
                (dn2, got.at[5], 3),
            ):
                pl.when(cond)(lambda dst=dst, i=i: arrived(dst, ssem.at[i], rsem.at[i]))

        return go, finish

    go1, finish1 = exchange(st1, rv1, s1_s, s1_r)
    go1()

    arrived(gall.at[3], g_s.at[2], g_r.at[2])
    project(2)

    finish1()
    for b in range(3):
        x0, x1, x2 = st1[b], rv1[2 * b], rv1[2 * b + 1]
        top = jnp.maximum(jnp.maximum(x0, x1), x2)
        lse = top + jnp.log2(jnp.exp2(x0 - top) + jnp.exp2(x1 - top) + jnp.exp2(x2 - top))
        c = jnp.exp2(m_loc[b] - lse)
        c_row[b] = c
        c_col[b] = jnp.transpose(c)

    def delta_block(b, g):
        for n in range(heads):
            col = c_col[b, :, pl.ds(4 * g + n, 1)]
            d = (q_block(dx, b, g, n).astype(F32) * col).astype(BF16)
            dscaled[b, g, n] = d
            total = jnp.zeros((8, lanes), F32)
            for i in range(chunks):
                rows = pl.ds((i % (chunks // 2)) * chunk, chunk)
                dp = dot_nt(vb[i // (chunks // 2), rows, head(n)], d)
                krows = pl.ds(i * chunk, chunk)
                dprobs[b, g, n, krows] = dp
                x = dp * probs[b, g, n, krows].astype(F32)
                total = total + jnp.sum(x.reshape(chunk // 8, 8, lanes), axis=0)
            st2[g, b, pl.ds(n, 1)] = jnp.sum(total, axis=0, keepdims=True)

    def value_block(b, g):
        for n in range(heads):
            dv_acc[n] += dot(probs[b, g, n], dscaled[b, g, n])

    def score_grad_block(b, g):
        delta = st2[g, b] + rv2[g, 2 * b] + rv2[g, 2 * b + 1]
        for n in range(heads):
            shift = delta[n : n + 1] * c_row[b, pl.ds(4 * g + n, 1)]
            ds = (probs[b, g, n].astype(F32) * (dprobs[b, g, n] - shift)).astype(BF16)
            dqt = dot(kt[n], ds) * SCALE
            dq = jnp.transpose(dqt).astype(BF16)
            dq_part[b, g, :, :, head(n)] = dq.reshape(2, grp, HD)
            dk_acc[n] += dot(ds, q_block(qx, b, g, n))

    ex2 = [exchange(st2.at[g], rv2.at[g], s2_s.at[g], s2_r.at[g]) for g in range(2)]

    def p_send(j, g, tq):
        return remote(
            dq_part.at[2 * j, g, tq],
            dq_in.at[t, 2 - 2 * j, g],
            p_s.at[g, j, tq],
            p_r.at[g, 1 - j, t],
            (tq, h - 1 + 2 * j, y),
        )

    def p_sib(g):
        return remote(dq_part.at[1, g, 1 - t], dq_in.at[t, 1, g], p_s.at[g, 2, 0], p_r.at[g, 2, 0], sib)

    def grads(g):
        @pl.loop(0, 2)
        def _(j):
            score_grad_block(2 * j, g)
            hh = h - 1 + 2 * j

            @pl.when((hh >= 0) & (hh < heights))
            def _():
                for tq in range(2):
                    p_send(j, g, tq).start()

        score_grad_block(1, g)
        p_sib(g).start()
        dq_in[t, 1, g] = dq_part[1, g, t]

    d_wait(0)

    @pl.loop(0, 3)
    def _(b):
        delta_block(b, 0)

    ex2[0][0]()

    @pl.loop(0, 3)
    def _(b):
        value_block(b, 0)

    d_wait(1)
    d_wait(2)

    @pl.loop(0, 3)
    def _(b):
        delta_block(b, 1)

    ex2[1][0]()
    ex2[0][1]()
    grads(0)

    @pl.loop(0, 3)
    def _(b):
        value_block(b, 1)

    for n in range(heads):
        dv_low[:, :, head(n)] = dv_acc[n].astype(BF16).reshape(2, tile, HD)
    dv_sib = remote(dv_low.at[1 - t], dv_hbm.at[:, mine], e_s.at[0], e_r.at[0], sib)
    dv_sib.start()
    dv_out = pltpu.make_async_copy(dv_low.at[t], dv_hbm.at[:, mine], osem.at[0])
    dv_out.start()

    ex2[1][1]()
    grads(1)

    for n in range(heads):
        dk_low[:, :, head(n)] = (dk_acc[n] * SCALE).astype(BF16).reshape(2, tile, HD)
    dk_sib = remote(dk_low.at[1 - t], dk_hbm.at[:, mine], e_s.at[1], e_r.at[1], sib)
    dk_sib.start()
    dk_out = pltpu.make_async_copy(dk_low.at[t], dk_hbm.at[:, mine], osem.at[1])
    dk_out.start()

    for g in range(2):
        arrived(dq_in.at[1 - t, 1, g], p_s.at[g, 2, 0], p_r.at[g, 2, 0])
        both(
            lambda d, g=g: [
                arrived(dq_in.at[c, 2 * d, g], p_s.at[g, d, c], p_r.at[g, d, c]) for c in range(2)
            ]
        )
        for c in range(2):
            x = dq_in[c, 0, g].astype(F32) + dq_in[c, 1, g].astype(F32) + dq_in[c, 2, g].astype(F32)
            dq_out[g, :, part(c)] = x.astype(BF16)
        for k in (2 * g, 2 * g + 1):
            pltpu.make_async_copy(slot_of(dq_out, k), dq_hbm.at[rows_of(k)], osem.at[2 + k]).start()

    for cp in g_sends + sib_sends:
        cp.wait_send()
    both(lambda d: [q_send(c, d).wait_send() for c in range(2)])
    for i in range(3):
        both(lambda d, i=i: [d_send(i, c, d).wait_send() for c in range(2)])
        d_sib(i).wait_send()
    for g in range(2):
        both(lambda d, g=g: [p_send(d, g, tq).wait_send() for tq in range(2)])
        p_sib(g).wait_send()
    dv_sib.wait_send()
    dk_sib.wait_send()
    arrived(dv_hbm.at[:, other], e_s.at[0], e_r.at[0])
    arrived(dk_hbm.at[:, other], e_s.at[1], e_r.at[1])
    dv_out.wait()
    dk_out.wait()
    for k in range(4):
        pltpu.make_async_copy(slot_of(dq_out, k), dq_hbm.at[rows_of(k)], osem.at[2 + k]).wait()


def hand_over(a, b, c, x, y, z):
    x[...] = a[...]
    y[...] = b[...]
    z[...] = c[...]


def local(queries, key_rows, value_rows, grad_output, out_weight, window_flags, valid_counts):
    tile, width = queries.shape[3:]
    model = grad_output.shape[-1]
    half = width // 2
    heads = half // HD
    grp, shard = tile // 2, tile // 4
    lanes, nk = 2 * grp, 2 * tile
    heights = lax.axis_size("height")
    shape = jax.ShapeDtypeStruct((tile, width), BF16)
    any_spec = pl.BlockSpec(memory_space=pl.ANY)
    dma = pltpu.SemaphoreType.DMA
    vm = pltpu.VMEM
    outs = pl.pallas_call(
        lambda *refs: kernel(heights, *refs),
        out_shape=(shape, shape, shape),
        in_specs=[any_spec] * 7,
        out_specs=(any_spec, any_spec, any_spec),
        scratch_shapes=[
            vm((2, 9, 1, heights), jnp.int32),
            vm((2, 1, heights), jnp.int32),
            vm((2, grp, width), BF16),
            vm((2, grp, width), BF16),
            vm((4, shard, model), BF16),
            vm((width, model), BF16),
            vm((3, 2, 2, grp, half), BF16),
            vm((3, 2, 2, grp, half), BF16),
            vm((2, tile, half), BF16),
            vm((2, tile, half), BF16),
            vm((heads, HD, nk), BF16),
            vm((3, nk, lanes), F32),
            vm((nk, lanes), F32),
            vm((3, 2, heads, nk, lanes), BF16),
            vm((3, 2, heads, nk, lanes), F32),
            vm((3, 2, heads, lanes, HD), BF16),
            vm((heads, nk, HD), F32),
            vm((heads, nk, HD), F32),
            vm((2, tile, half), BF16),
            vm((2, tile, half), BF16),
            vm((3, 2, 2, grp, half), BF16),
            vm((2, 3, 2, grp, half), BF16),
            vm((2, grp, width), BF16),
            vm((3, 8, lanes), F32),
            vm((6, 8, lanes), F32),
            vm((3, 8, lanes), F32),
            vm((3, 8, lanes), F32),
            vm((3, lanes, 8), F32),
            vm((2, 3, 8, lanes), F32),
            vm((2, 6, 8, lanes), F32),
            dma((14,)),
            dma((6,)),
            dma((3,)),
            dma((3,)),
            dma((2, 2)),
            dma((2, 2)),
            dma((3,)),
            dma((3,)),
            dma((3, 3, 2)),
            dma((3, 3, 2)),
            dma((4,)),
            dma((4,)),
            dma((2, 4)),
            dma((2, 4)),
            dma((2, 3, 2)),
            dma((2, 3, 2)),
            dma((2,)),
            dma((2,)),
        ],
        compiler_params=pltpu.CompilerParams(
            collective_id=0, has_side_effects=True, vmem_limit_bytes=56 * 2**20
        ),
    )(
        window_flags.transpose(0, 3, 2, 1),
        valid_counts.transpose(0, 2, 1),
        queries.reshape(tile, width),
        key_rows.reshape(tile, width),
        value_rows.reshape(tile, width),
        grad_output.reshape(grad_output.shape[3], model),
        out_weight,
    )
    outs = pl.pallas_call(hand_over, out_shape=(shape, shape, shape))(*outs)
    return tuple(x.reshape(queries.shape) for x in outs)


def solution(mesh):
    wide = P("tm", "height", None, None, "tensor")
    placed = (wide, wide, wide, P("tm", "height", None, "tensor", None), P("tensor", None), P(), P())
    return jax.shard_map(local, mesh=mesh, in_specs=placed, out_specs=(wide, wide, wide), check_vma=False)
```

```python
import jax
import jax.numpy as jnp
from jax import lax
from jax.experimental import pallas as pl
from jax.experimental.pallas import tpu as pltpu
from jax.sharding import PartitionSpec as P

HD = 128
SCALE = HD ** (-0.5)
LOG2E = 1.4426950408889634
MASKED = -1e30
FLOOR = -1e25
MESH = pl.DeviceIdType.MESH
F32 = jnp.float32
BF16 = jnp.bfloat16
SHARD = (0, 1, 3, 2)
NT = (((1,), (1,)), ((), ()))


def dot(a, b):
    return jnp.dot(a, b, preferred_element_type=F32)


def dot_nt(a, b):
    return lax.dot_general(a, b, NT, preferred_element_type=F32)


def kernel(
    heights,
    f_hbm,
    n_hbm,
    q_hbm,
    k_hbm,
    v_hbm,
    g_hbm,
    w_hbm,
    parts,
    dk_hbm,
    dv_hbm,
    flags,
    counts,
    qown,
    down,
    gall,
    wall,
    qx,
    dx,
    kb,
    vb,
    kt,
    bias,
    sbuf,
    probs,
    dprobs,
    dscaled,
    dk_acc,
    dv_acc,
    dk_low,
    dv_low,
    dq_part,
    st1,
    rv1,
    m_loc,
    c_row,
    c_col,
    st2,
    rv2,
    lsem,
    osem,
    g_s,
    g_r,
    q_s,
    q_r,
    sib_s,
    sib_r,
    d_s,
    d_r,
    s1_s,
    s1_r,
    s2_s,
    s2_r,
    p_s,
    p_r,
    e_s,
    e_r,
):
    t = lax.axis_index("tm")
    h = lax.axis_index("height")
    y = lax.axis_index("tensor")
    half = k_hbm.shape[1] // 2
    heads = half // HD
    tile = k_hbm.shape[0]
    grp = tile // 2
    shard = tile // 4
    lanes = 2 * grp
    sib = (1 - t, h, y)
    up, dn, up2, dn2 = h > 0, h < heights - 1, h > 1, h < heights - 2
    mine = pl.ds(pl.multiple_of(t * half, HD), half)
    other = pl.ds(pl.multiple_of((1 - t) * half, HD), half)

    def rows_of(k):
        return pl.ds(pl.multiple_of(lax.rem(y + SHARD[k], 4) * shard, shard), shard)

    def slot_of(ref, k):
        return ref.at[k // 2, pl.ds((k % 2) * shard, shard)]

    def remote(src, dst, ssem, rsem, dev):
        return pltpu.make_async_remote_copy(
            src_ref=src, dst_ref=dst, send_sem=ssem, recv_sem=rsem, device_id=dev, device_id_type=MESH
        )

    def arrived(dst, ssem, rsem):
        remote(dst, dst, ssem, rsem, sib).wait_recv()

    def sent(src, ssem, rsem):
        remote(src, src, ssem, rsem, sib).wait_send()

    q_loads = [pltpu.make_async_copy(q_hbm.at[rows_of(k)], slot_of(qown, k), lsem.at[k]) for k in range(4)]
    g_load = pltpu.make_async_copy(g_hbm, gall.at[0], lsem.at[4])
    k_load = pltpu.make_async_copy(k_hbm.at[:, mine], kb.at[t], lsem.at[5])
    v_load = pltpu.make_async_copy(v_hbm.at[:, mine], vb.at[t], lsem.at[6])
    w_load = pltpu.make_async_copy(w_hbm, wall, lsem.at[7])
    f_load = pltpu.make_async_copy(f_hbm, flags, lsem.at[13])
    n_load = pltpu.make_async_copy(n_hbm, counts, lsem.at[14])
    f_load.start()
    n_load.start()
    g_load.start()
    for cp in q_loads:
        cp.start()
    k_load.start()
    v_load.start()
    w_load.start()

    barrier = pltpu.get_barrier_semaphore()

    def greet(dev):
        pl.semaphore_signal(barrier, inc=1, device_id=dev, device_id_type=MESH)

    greet(sib)
    for k in (1, 2, 3):
        greet((t, h, lax.rem(y + k, 4)))

    @pl.when(up)
    def _():
        greet((0, h - 1, y))
        greet((1, h - 1, y))

    @pl.when(dn)
    def _():
        greet((0, h + 1, y))
        greet((1, h + 1, y))

    @pl.when(up2)
    def _():
        greet((t, h - 2, y))

    @pl.when(dn2)
    def _():
        greet((t, h + 2, y))

    def zero_part(b):
        return pltpu.make_async_copy(dx.at[b], parts.at[:, b], osem.at[2])

    def absent(b):
        qx[b] = jnp.zeros(qx.shape[1:], BF16)
        dx[b] = jnp.zeros(dx.shape[1:], BF16)
        zero_part(b).start()

    nothing = jnp.full((8, lanes), FLOOR, F32)
    zeros = jnp.zeros((8, lanes), F32)

    def absent_stats(i):
        rv1[i] = nothing
        rv2[0, i] = zeros
        rv2[1, i] = zeros

    @pl.when(h == 0)
    def _():
        absent(0)
        absent_stats(1)
        absent_stats(2)

    @pl.when(h == heights - 1)
    def _():
        absent(2)
        absent_stats(3)
        absent_stats(4)

    @pl.when(h <= 1)
    def _():
        absent_stats(0)

    @pl.when(h >= heights - 2)
    def _():
        absent_stats(5)

    for b in range(3):
        st1[b] = zeros
        m_loc[b] = zeros
        st2[0, b] = zeros
        st2[1, b] = zeros
    dk_acc[...] = jnp.zeros(dk_acc.shape, F32)
    dv_acc[...] = jnp.zeros(dv_acc.shape, F32)

    f_load.wait()
    n_load.wait()
    position = lax.broadcasted_iota(jnp.int32, (tile, grp), 0).astype(F32)
    lane = lax.broadcasted_iota(jnp.int32, (1, heights), 1)

    def at_height(row, i):
        return jnp.sum(jnp.where(lane == i, row.astype(F32), 0.0), axis=1, keepdims=True)

    for b in range(3):
        hq = h + b - 1
        inside = (hq >= 0) & (hq < heights)
        hq = jnp.clip(hq, 0, heights - 1)
        for tq in range(2):
            for tk in range(2):
                flag = at_height(flags[tq, 3 * (tk - tq + 1) + 2 - b], hq)
                count = jnp.where(inside & (flag > 0.0), at_height(counts[tk], h), 0.0)
                bias[b, pl.ds(tk * tile, tile), pl.ds(tq * grp, grp)] = jnp.where(
                    position < count, 0.0, MASKED
                ).astype(F32)

    pl.semaphore_wait(
        barrier,
        4
        + 2 * up.astype(jnp.int32)
        + 2 * dn.astype(jnp.int32)
        + up2.astype(jnp.int32)
        + dn2.astype(jnp.int32),
    )

    g_load.wait()
    ahead, behind = (t, h, lax.rem(y + 1, 4)), (t, h, lax.rem(y + 3, 4))
    first, second = pl.ds(0, shard // 2), pl.ds(shard // 2, shard // 2)
    g_sends = [
        remote(gall.at[0, first], gall.at[2, first], g_s.at[0], g_r.at[0], ahead),
        remote(gall.at[0, second], gall.at[1, second], g_s.at[1], g_r.at[1], behind),
        remote(gall.at[0, second], gall.at[2, second], g_s.at[2], g_r.at[2], ahead),
        remote(gall.at[0, first], gall.at[1, first], g_s.at[3], g_r.at[3], behind),
    ]
    g_relays = [
        remote(gall.at[2, first], gall.at[3, first], g_s.at[4], g_r.at[4], ahead),
        remote(gall.at[1, second], gall.at[3, second], g_s.at[5], g_r.at[5], behind),
    ]
    for cp in g_sends:
        cp.start()
    for cp in q_loads:
        cp.wait()
    sib_sends = [
        remote(k_hbm.at[:, other], kb.at[t], sib_s.at[0], sib_r.at[0], sib),
        remote(v_hbm.at[:, other], vb.at[t], sib_s.at[1], sib_r.at[1], sib),
        remote(qown.at[:, :, other], qx.at[1, :, t], sib_s.at[2], sib_r.at[2], sib),
    ]
    for cp in sib_sends:
        cp.start()

    def part(c):
        return pl.ds(c * half, half)

    def q_send(c, d):
        return remote(
            qown.at[:, :, part(c)], qx.at[2 - 2 * d, :, t], q_s.at[d, c], q_r.at[1 - d, t], (c, h - 1 + 2 * d, y)
        )

    def both(fn):
        @pl.when(up)
        def _():
            fn(0)

        @pl.when(dn)
        def _():
            fn(1)

    both(lambda d: [q_send(c, d).start() for c in range(2)])
    q_copy = pltpu.make_async_copy(qown.at[:, :, mine], qx.at[1, :, t], lsem.at[8])
    q_copy.start()

    chunk = 128
    nk = 2 * tile
    chunks = nk // chunk

    def head(n):
        return pl.ds(n * HD, HD)

    def q_block(ref, b, g, n):
        return ref[b, g, :, :, head(n)].reshape(lanes, HD)

    def score_block(b):
        for g in range(2):
            for n in range(heads):
                qv = q_block(qx, b, g, n)
                top = jnp.full((8, lanes), FLOOR, F32)
                for i in range(chunks):
                    rows = pl.ds((i % (chunks // 2)) * chunk, chunk)
                    s = dot_nt(kb[i // (chunks // 2), rows, head(n)], qv) * (SCALE * LOG2E)
                    s = s + bias[b, pl.ds(i * chunk, chunk)]
                    sbuf[pl.ds(i * chunk, chunk)] = s
                    top = jnp.maximum(top, jnp.max(s.reshape(chunk // 8, 8, lanes), axis=0))
                m = jnp.max(top, axis=0, keepdims=True)
                total = jnp.zeros((8, lanes), F32)
                for i in range(chunks):
                    e = jnp.exp2(sbuf[pl.ds(i * chunk, chunk)] - m)
                    total = total + jnp.sum(e.reshape(chunk // 8, 8, lanes), axis=0)
                    probs[b, g, n, pl.ds(i * chunk, chunk)] = e.astype(BF16)
                total = jnp.sum(total, axis=0, keepdims=True)
                r = pl.ds(4 * g + n, 1)
                m_loc[b, r] = m
                st1[b, r] = m + jnp.log2(jnp.maximum(total, 1e-37))

    k_load.wait()
    v_load.wait()
    q_copy.wait()
    arrived(kb.at[1 - t], sib_s.at[0], sib_r.at[0])
    arrived(vb.at[1 - t], sib_s.at[1], sib_r.at[1])
    arrived(qx.at[1, :, 1 - t], sib_s.at[2], sib_r.at[2])
    for n in range(heads):
        kt[n] = jnp.transpose(kb[:, :, head(n)].reshape(nk, HD))
    score_block(1)

    w_load.wait()

    def d_send(i, c, d):
        src, dst = d_ref(i)
        return remote(
            src.at[:, part(c)], dst(2 - 2 * d), d_s.at[i, d, c], d_r.at[i, 1 - d, t], (c, h - 1 + 2 * d, y)
        )

    def d_region(i):
        return i // 2, pl.ds((i % 2) * shard, shard)

    def d_ref(i):
        g, rows = d_region(i)
        return down.at[g, rows], lambda b: dx.at[b, g, t, rows]

    def d_sib(i):
        g, rows = d_region(i)
        return remote(
            down.at[g, rows, other], dx.at[1, g, t, rows], d_s.at[i, 2, 0], d_r.at[i, 2, 0], sib
        )

    def project(i):
        g, rows = d_region(i)
        down[g, rows] = dot_nt(gall[i], wall[...]).astype(BF16)
        both(lambda d: [d_send(i, c, d).start() for c in range(2)])
        d_sib(i).start()
        pltpu.make_async_copy(down.at[g, rows, mine], dx.at[1, g, t, rows], lsem.at[9 + i]).start()

    def d_wait(i):
        g, rows = d_region(i)
        pltpu.make_async_copy(down.at[g, rows, mine], dx.at[1, g, t, rows], lsem.at[9 + i]).wait()
        arrived(dx.at[1, g, 1 - t, rows], d_s.at[i, 2, 0], d_r.at[i, 2, 0])
        both(
            lambda d: [
                arrived(dx.at[2 * d, g, tq, rows], d_s.at[i, d, tq], d_r.at[i, d, tq]) for tq in range(2)
            ]
        )

    project(0)
    arrived(gall.at[2, first], g_s.at[0], g_r.at[0])
    g_relays[0].start()
    arrived(gall.at[1, second], g_s.at[1], g_r.at[1])
    g_relays[1].start()
    arrived(gall.at[1, first], g_s.at[3], g_r.at[3])
    project(1)
    arrived(gall.at[2, second], g_s.at[2], g_r.at[2])
    project(2)

    both(lambda d: [arrived(qx.at[2 * d, :, tq], q_s.at[d, tq], q_r.at[d, tq]) for tq in range(2)])

    @pl.loop(0, 2)
    def _(j):
        score_block(2 * j)

    def exchange(own, got, ssem, rsem):
        def copies():
            return (
                (up, remote(own.at[pl.ds(0, 2)], got.at[pl.ds(3, 2)], ssem.at[0], rsem.at[1], (t, h - 1, y))),
                (dn, remote(own.at[pl.ds(1, 2)], got.at[pl.ds(1, 2)], ssem.at[1], rsem.at[0], (t, h + 1, y))),
                (up2, remote(own.at[0], got.at[5], ssem.at[2], rsem.at[3], (t, h - 2, y))),
                (dn2, remote(own.at[2], got.at[0], ssem.at[3], rsem.at[2], (t, h + 2, y))),
            )

        def go():
            for cond, cp in copies():
                pl.when(cond)(cp.start)

        def finish():
            for cond, cp in copies():
                pl.when(cond)(cp.wait_send)
            for cond, dst, i in (
                (up, got.at[pl.ds(1, 2)], 0),
                (dn, got.at[pl.ds(3, 2)], 1),
                (up2, got.at[0], 2),
                (dn2, got.at[5], 3),
            ):
                pl.when(cond)(lambda dst=dst, i=i: arrived(dst, ssem.at[i], rsem.at[i]))

        return go, finish

    go1, finish1 = exchange(st1, rv1, s1_s, s1_r)
    go1()

    arrived(gall.at[3, first], g_s.at[4], g_r.at[4])
    arrived(gall.at[3, second], g_s.at[5], g_r.at[5])
    project(3)

    finish1()
    for b in range(3):
        x0, x1, x2 = st1[b], rv1[2 * b], rv1[2 * b + 1]
        top = jnp.maximum(jnp.maximum(x0, x1), x2)
        lse = top + jnp.log2(jnp.exp2(x0 - top) + jnp.exp2(x1 - top) + jnp.exp2(x2 - top))
        c = jnp.exp2(m_loc[b] - lse)
        c_row[b] = c
        c_col[b] = jnp.transpose(c)

    def delta_block(b, g):
        for n in range(heads):
            col = c_col[b, :, pl.ds(4 * g + n, 1)]
            d = (q_block(dx, b, g, n).astype(F32) * col).astype(BF16)
            dscaled[b, g, n] = d
            total = jnp.zeros((8, lanes), F32)
            for i in range(chunks):
                rows = pl.ds((i % (chunks // 2)) * chunk, chunk)
                dp = dot_nt(vb[i // (chunks // 2), rows, head(n)], d)
                krows = pl.ds(i * chunk, chunk)
                dprobs[b, g, n, krows] = dp
                x = dp * probs[b, g, n, krows].astype(F32)
                total = total + jnp.sum(x.reshape(chunk // 8, 8, lanes), axis=0)
            st2[g, b, pl.ds(n, 1)] = jnp.sum(total, axis=0, keepdims=True)

    def value_block(b, g):
        for n in range(heads):
            dv_acc[n] += dot(probs[b, g, n], dscaled[b, g, n])

    def score_grad_block(b, g):
        delta = st2[g, b] + rv2[g, 2 * b] + rv2[g, 2 * b + 1]
        for n in range(heads):
            shift = delta[n : n + 1] * c_row[b, pl.ds(4 * g + n, 1)]
            ds = (probs[b, g, n].astype(F32) * (dprobs[b, g, n] - shift)).astype(BF16)
            dqt = dot(kt[n], ds) * SCALE
            dq = jnp.transpose(dqt).astype(BF16)
            dq_part[b, g, :, :, head(n)] = dq.reshape(2, grp, HD)
            dk_acc[n] += dot(ds, q_block(qx, b, g, n))

    ex2 = [exchange(st2.at[g], rv2.at[g], s2_s.at[g], s2_r.at[g]) for g in range(2)]

    def p_send(j, g, tq):
        return remote(
            dq_part.at[2 * j, g, tq],
            parts.at[t, 2 - 2 * j, g],
            p_s.at[g, j, tq],
            p_r.at[g, 1 - j, t],
            (tq, h - 1 + 2 * j, y),
        )

    def p_sib(g):
        return remote(dq_part.at[1, g, 1 - t], parts.at[t, 1, g], p_s.at[g, 2, 0], p_r.at[g, 2, 0], sib)

    def p_own(g):
        return pltpu.make_async_copy(dq_part.at[1, g, t], parts.at[t, 1, g], osem.at[3 + g])

    def grads(g):
        @pl.loop(0, 2)
        def _(j):
            score_grad_block(2 * j, g)
            hh = h - 1 + 2 * j

            @pl.when((hh >= 0) & (hh < heights))
            def _():
                for tq in range(2):
                    p_send(j, g, tq).start()

        score_grad_block(1, g)
        p_sib(g).start()
        p_own(g).start()

    d_wait(0)
    d_wait(1)

    @pl.loop(0, 3)
    def _(b):
        delta_block(b, 0)

    ex2[0][0]()

    @pl.loop(0, 3)
    def _(b):
        value_block(b, 0)

    d_wait(2)
    d_wait(3)

    @pl.loop(0, 3)
    def _(b):
        delta_block(b, 1)

    ex2[1][0]()
    ex2[0][1]()
    grads(0)

    @pl.loop(0, 3)
    def _(b):
        value_block(b, 1)

    for n in range(heads):
        dv_low[:, :, head(n)] = dv_acc[n].astype(BF16).reshape(2, tile, HD)
    dv_sib = remote(dv_low.at[1 - t], dv_hbm.at[:, mine], e_s.at[0], e_r.at[0], sib)
    dv_sib.start()
    dv_out = pltpu.make_async_copy(dv_low.at[t], dv_hbm.at[:, mine], osem.at[0])
    dv_out.start()

    ex2[1][1]()
    grads(1)

    for n in range(heads):
        dk_low[:, :, head(n)] = (dk_acc[n] * SCALE).astype(BF16).reshape(2, tile, HD)
    dk_sib = remote(dk_low.at[1 - t], dk_hbm.at[:, mine], e_s.at[1], e_r.at[1], sib)
    dk_sib.start()
    dk_out = pltpu.make_async_copy(dk_low.at[t], dk_hbm.at[:, mine], osem.at[1])
    dk_out.start()

    for g in range(2):
        p_own(g).wait()
        arrived(parts.at[1 - t, 1, g], p_s.at[g, 2, 0], p_r.at[g, 2, 0])
        both(
            lambda d, g=g: [
                arrived(parts.at[c, 2 * d, g], p_s.at[g, d, c], p_r.at[g, d, c]) for c in range(2)
            ]
        )
    pl.when(h == 0)(zero_part(0).wait)
    pl.when(h == heights - 1)(zero_part(2).wait)

    for cp in g_sends + g_relays + sib_sends:
        cp.wait_send()
    both(lambda d: [q_send(c, d).wait_send() for c in range(2)])
    for i in range(4):
        both(lambda d, i=i: [d_send(i, c, d).wait_send() for c in range(2)])
        d_sib(i).wait_send()
    for g in range(2):
        both(lambda d, g=g: [p_send(d, g, tq).wait_send() for tq in range(2)])
        p_sib(g).wait_send()
    dv_sib.wait_send()
    dk_sib.wait_send()
    arrived(dv_hbm.at[:, other], e_s.at[0], e_r.at[0])
    arrived(dk_hbm.at[:, other], e_s.at[1], e_r.at[1])
    dv_out.wait()
    dk_out.wait()


def finish(parts, dk, dv, dq_hbm, dk_hbm, dv_hbm, buf, dk_buf, dv_buf, dq_out, sem):
    y = lax.axis_index("tensor")
    grp, half = buf.shape[3:]
    shard = grp // 2
    loads = [
        pltpu.make_async_copy(parts.at[:, :, 0], buf.at[0], sem.at[0]),
        pltpu.make_async_copy(parts.at[:, :, 1], buf.at[1], sem.at[1]),
        pltpu.make_async_copy(dk, dk_buf, sem.at[2]),
        pltpu.make_async_copy(dv, dv_buf, sem.at[3]),
    ]
    stores = [
        pltpu.make_async_copy(dk_buf, dk_hbm, sem.at[4]),
        pltpu.make_async_copy(dv_buf, dv_hbm, sem.at[5]),
    ]
    for k in range(4):
        rows = pl.ds(pl.multiple_of(lax.rem(y + SHARD[k], 4) * shard, shard), shard)
        stores.append(
            pltpu.make_async_copy(
                dq_out.at[k // 2, pl.ds((k % 2) * shard, shard)], dq_hbm.at[rows], sem.at[6 + k]
            )
        )
    for cp in loads:
        cp.start()
    for g in range(2):
        loads[g].wait()
        for c in range(2):
            x = buf[g, c, 0].astype(F32) + buf[g, c, 1].astype(F32) + buf[g, c, 2].astype(F32)
            dq_out[g, :, pl.ds(c * half, half)] = x.astype(BF16)
        stores[2 + 2 * g].start()
        stores[3 + 2 * g].start()
    for i in range(2):
        loads[2 + i].wait()
        stores[i].start()
    for cp in stores:
        cp.wait()


def local(queries, key_rows, value_rows, grad_output, out_weight, window_flags, valid_counts):
    tile, width = queries.shape[3:]
    model = grad_output.shape[-1]
    half = width // 2
    heads = half // HD
    grp, shard = tile // 2, tile // 4
    lanes, nk = 2 * grp, 2 * tile
    heights = lax.axis_size("height")
    shape = jax.ShapeDtypeStruct((tile, width), BF16)
    parts_shape = jax.ShapeDtypeStruct((2, 3, 2, grp, half), BF16)
    any_spec = pl.BlockSpec(memory_space=pl.ANY)
    dma = pltpu.SemaphoreType.DMA
    vm = pltpu.VMEM
    outs = pl.pallas_call(
        lambda *refs: kernel(heights, *refs),
        out_shape=(parts_shape, shape, shape),
        in_specs=[any_spec] * 7,
        out_specs=(any_spec, any_spec, any_spec),
        scratch_shapes=[
            vm((2, 9, 1, heights), jnp.int32),
            vm((2, 1, heights), jnp.int32),
            vm((2, grp, width), BF16),
            vm((2, grp, width), BF16),
            vm((4, shard, model), BF16),
            vm((width, model), BF16),
            vm((3, 2, 2, grp, half), BF16),
            vm((3, 2, 2, grp, half), BF16),
            vm((2, tile, half), BF16),
            vm((2, tile, half), BF16),
            vm((heads, HD, nk), BF16),
            vm((3, nk, lanes), F32),
            vm((nk, lanes), F32),
            vm((3, 2, heads, nk, lanes), BF16),
            vm((3, 2, heads, nk, lanes), F32),
            vm((3, 2, heads, lanes, HD), BF16),
            vm((heads, nk, HD), F32),
            vm((heads, nk, HD), F32),
            vm((2, tile, half), BF16),
            vm((2, tile, half), BF16),
            vm((3, 2, 2, grp, half), BF16),
            vm((3, 8, lanes), F32),
            vm((6, 8, lanes), F32),
            vm((3, 8, lanes), F32),
            vm((3, 8, lanes), F32),
            vm((3, lanes, 8), F32),
            vm((2, 3, 8, lanes), F32),
            vm((2, 6, 8, lanes), F32),
            dma((15,)),
            dma((6,)),
            dma((6,)),
            dma((6,)),
            dma((2, 2)),
            dma((2, 2)),
            dma((3,)),
            dma((3,)),
            dma((4, 3, 2)),
            dma((4, 3, 2)),
            dma((4,)),
            dma((4,)),
            dma((2, 4)),
            dma((2, 4)),
            dma((2, 3, 2)),
            dma((2, 3, 2)),
            dma((2,)),
            dma((2,)),
        ],
        compiler_params=pltpu.CompilerParams(
            collective_id=0, has_side_effects=True, vmem_limit_bytes=56 * 2**20
        ),
    )(
        window_flags.transpose(0, 3, 2, 1),
        valid_counts.transpose(0, 2, 1),
        queries.reshape(tile, width),
        key_rows.reshape(tile, width),
        value_rows.reshape(tile, width),
        grad_output.reshape(grad_output.shape[3], model),
        out_weight,
    )
    outs = pl.pallas_call(
        finish,
        out_shape=(shape, shape, shape),
        in_specs=[any_spec] * 3,
        out_specs=(any_spec,) * 3,
        scratch_shapes=[
            vm((2, 2, 3, grp, half), BF16),
            vm((tile, width), BF16),
            vm((tile, width), BF16),
            vm((2, grp, width), BF16),
            dma((10,)),
        ],
    )(*outs)
    return tuple(x.reshape(queries.shape) for x in outs)


def solution(mesh):
    wide = P("tm", "height", None, None, "tensor")
    placed = (wide, wide, wide, P("tm", "height", None, "tensor", None), P("tensor", None), P(), P())
    return jax.shard_map(local, mesh=mesh, in_specs=placed, out_specs=(wide, wide, wide), check_vma=False)
```

```python
import jax
import jax.numpy as jnp
from jax import lax
from jax.experimental import pallas as pl
from jax.experimental.pallas import tpu as pltpu
from jax.sharding import PartitionSpec as P

HD = 128
SCALE = HD ** (-0.5)
LOG2E = 1.4426950408889634
MASKED = -1e30
FLOOR = -1e25
MESH = pl.DeviceIdType.MESH
F32 = jnp.float32
BF16 = jnp.bfloat16
SHARD = (0, 1, 3, 2)
NT = (((1,), (1,)), ((), ()))


def dot(a, b):
    return jnp.dot(a, b, preferred_element_type=F32)


def dot_nt(a, b):
    return lax.dot_general(a, b, NT, preferred_element_type=F32)


def kernel(
    heights,
    f_hbm,
    n_hbm,
    q_hbm,
    k_hbm,
    v_hbm,
    g_hbm,
    w_hbm,
    parts,
    dk_hbm,
    dv_hbm,
    flags,
    counts,
    qown,
    down,
    gall,
    wall,
    qx,
    dx,
    kb,
    vb,
    kt,
    bias,
    sbuf,
    probs,
    dprobs,
    dscores,
    dk_acc,
    dv_acc,
    dk_low,
    dv_low,
    dq_part,
    st,
    rv,
    loc,
    row,
    col,
    lsem,
    osem,
    g_s,
    g_r,
    q_s,
    q_r,
    sib_s,
    sib_r,
    d_s,
    d_r,
    st_s,
    st_r,
    p_s,
    p_r,
    e_s,
    e_r,
):
    t = lax.axis_index("tm")
    h = lax.axis_index("height")
    y = lax.axis_index("tensor")
    half = k_hbm.shape[1] // 2
    heads = half // HD
    tile = k_hbm.shape[0]
    shard = tile // 4
    pair = 2 * shard
    lanes = 2 * pair
    sib = (1 - t, h, y)
    up, dn, up2, dn2 = h > 0, h < heights - 1, h > 1, h < heights - 2
    mine = pl.ds(pl.multiple_of(t * half, HD), half)
    other = pl.ds(pl.multiple_of((1 - t) * half, HD), half)

    def rows_of(k):
        return pl.ds(pl.multiple_of(lax.rem(y + SHARD[k], 4) * shard, shard), shard)

    def remote(src, dst, ssem, rsem, dev):
        return pltpu.make_async_remote_copy(
            src_ref=src, dst_ref=dst, send_sem=ssem, recv_sem=rsem, device_id=dev, device_id_type=MESH
        )

    def arrived(dst, ssem, rsem):
        remote(dst, dst, ssem, rsem, sib).wait_recv()

    def sent(src, ssem, rsem):
        remote(src, src, ssem, rsem, sib).wait_send()

    q_loads = [pltpu.make_async_copy(q_hbm.at[rows_of(k)], qown.at[k], lsem.at[k]) for k in range(4)]
    g_load = pltpu.make_async_copy(g_hbm, gall.at[0], lsem.at[4])
    k_load = pltpu.make_async_copy(k_hbm.at[:, mine], kb.at[t], lsem.at[5])
    v_load = pltpu.make_async_copy(v_hbm.at[:, mine], vb.at[t], lsem.at[6])
    w_load = pltpu.make_async_copy(w_hbm, wall, lsem.at[7])
    f_load = pltpu.make_async_copy(f_hbm, flags, lsem.at[13])
    n_load = pltpu.make_async_copy(n_hbm, counts, lsem.at[14])
    f_load.start()
    n_load.start()
    g_load.start()
    for cp in q_loads:
        cp.start()
    k_load.start()
    v_load.start()
    w_load.start()

    barrier = pltpu.get_barrier_semaphore()

    def greet(dev):
        pl.semaphore_signal(barrier, inc=1, device_id=dev, device_id_type=MESH)

    greet(sib)
    for k in (1, 2, 3):
        greet((t, h, lax.rem(y + k, 4)))

    @pl.when(up)
    def _():
        greet((0, h - 1, y))
        greet((1, h - 1, y))

    @pl.when(dn)
    def _():
        greet((0, h + 1, y))
        greet((1, h + 1, y))

    @pl.when(up2)
    def _():
        greet((t, h - 2, y))

    @pl.when(dn2)
    def _():
        greet((t, h + 2, y))

    def zero_part(b, c):
        return pltpu.make_async_copy(dx.at[pl.ds(0, 4), b // 2, c], parts.at[c, b], osem.at[2 + c])

    def absent(b):
        for k in range(4):
            qx[k, b // 2] = jnp.zeros(qx.shape[2:], BF16)
            dx[k, b // 2] = jnp.zeros(dx.shape[2:], BF16)
        for c in range(2):
            zero_part(b, c).start()

    sub = lax.broadcasted_iota(jnp.int32, (8, pair), 0)
    nothing = jnp.where(sub < 4, FLOOR, 0.0).astype(F32)
    zeros = jnp.zeros((8, pair), F32)

    def absent_stats(i):
        for k in range(4):
            rv[k, i] = nothing

    @pl.when(h == 0)
    def _():
        absent(0)
        absent_stats(1)
        absent_stats(2)

    @pl.when(h == heights - 1)
    def _():
        absent(2)
        absent_stats(3)
        absent_stats(4)

    @pl.when(h <= 1)
    def _():
        absent_stats(0)

    @pl.when(h >= heights - 2)
    def _():
        absent_stats(5)

    for k in range(4):
        for b in range(3):
            st[k, b] = zeros
            loc[k, b] = zeros
    dk_acc[...] = jnp.zeros(dk_acc.shape, F32)
    dv_acc[...] = jnp.zeros(dv_acc.shape, F32)

    f_load.wait()
    n_load.wait()
    position = lax.broadcasted_iota(jnp.int32, (tile, pair), 0).astype(F32)
    late = lax.broadcasted_iota(jnp.int32, (1, pair), 1) >= shard
    lane = lax.broadcasted_iota(jnp.int32, (1, heights), 1)

    def at_height(values, i):
        return jnp.sum(jnp.where(lane == i, values.astype(F32), 0.0), axis=1, keepdims=True)

    for b in range(3):
        hq = h + b - 1
        inside = (hq >= 0) & (hq < heights)
        hq = jnp.clip(hq, 0, heights - 1)
        for tk in range(2):
            count = []
            for tq in range(2):
                flag = at_height(flags[tq, 3 * (tk - tq + 1) + 2 - b], hq)
                count.append(jnp.where(inside & (flag > 0.0), at_height(counts[tk], h), 0.0))
            limit = jnp.where(late, count[1], count[0])
            value = jnp.where(position < limit, 0.0, MASKED).astype(F32)
            krows = pl.ds(tk * tile, tile)
            if b == 1:
                bias[1, krows, pl.ds(0, pair)] = value
                bias[1, krows, pl.ds(pair, pair)] = value
            else:
                bias[0, krows, pl.ds((b // 2) * pair, pair)] = value

    pl.semaphore_wait(
        barrier,
        4
        + 2 * up.astype(jnp.int32)
        + 2 * dn.astype(jnp.int32)
        + up2.astype(jnp.int32)
        + dn2.astype(jnp.int32),
    )

    g_load.wait()
    ahead, behind = (t, h, lax.rem(y + 1, 4)), (t, h, lax.rem(y + 3, 4))
    first, second = pl.ds(0, shard // 2), pl.ds(shard // 2, shard // 2)
    g_sends = [
        remote(gall.at[0, first], gall.at[2, first], g_s.at[0], g_r.at[0], ahead),
        remote(gall.at[0, second], gall.at[1, second], g_s.at[1], g_r.at[1], behind),
        remote(gall.at[0, second], gall.at[2, second], g_s.at[2], g_r.at[2], ahead),
        remote(gall.at[0, first], gall.at[1, first], g_s.at[3], g_r.at[3], behind),
    ]
    g_relays = [
        remote(gall.at[2, first], gall.at[3, first], g_s.at[4], g_r.at[4], ahead),
        remote(gall.at[1, second], gall.at[3, second], g_s.at[5], g_r.at[5], behind),
    ]
    for cp in g_sends:
        cp.start()
    for cp in q_loads:
        cp.wait()
    sib_sends = [
        remote(k_hbm.at[:, other], kb.at[t], sib_s.at[0], sib_r.at[0], sib),
        remote(v_hbm.at[:, other], vb.at[t], sib_s.at[1], sib_r.at[1], sib),
        remote(qown.at[pl.ds(0, 2), :, other], qx.at[4, :, t], sib_s.at[2], sib_r.at[2], sib),
        remote(qown.at[pl.ds(2, 2), :, other], qx.at[5, :, t], sib_s.at[3], sib_r.at[3], sib),
    ]
    for cp in sib_sends:
        cp.start()

    def part(c):
        return pl.ds(c * half, half)

    def q_send(c, d):
        return remote(
            qown.at[:, :, part(c)],
            qx.at[pl.ds(0, 4), 1 - d, t],
            q_s.at[d, c],
            q_r.at[1 - d, t],
            (c, h - 1 + 2 * d, y),
        )

    def both(fn):
        @pl.when(up)
        def _():
            fn(0)

        @pl.when(dn)
        def _():
            fn(1)

    both(lambda d: [q_send(c, d).start() for c in range(2)])
    q_copies = [
        pltpu.make_async_copy(qown.at[pl.ds(2 * g, 2), :, mine], qx.at[4 + g, :, t], lsem.at[(8, 15)[g]])
        for g in range(2)
    ]
    for cp in q_copies:
        cp.start()

    chunk = 128
    nk = 2 * tile
    chunks = nk // chunk

    def head(n):
        return pl.ds(n * HD, HD)

    def rows_block(ref, u, n):
        return ref[u, :, :, :, head(n)].reshape(lanes, HD)

    def halo(s):
        return ((s, 0), (s, 2))

    def own(g):
        return ((2 * g, 1), (2 * g + 1, 1))

    def put(ref, places, r, value):
        for i, (s, b) in enumerate(places):
            ref[s, b, pl.ds(r, 1)] = value[:, i * pair : (i + 1) * pair]

    def score_block(u, places, which):
        for n in range(heads):
            qv = rows_block(qx, u, n)
            top = jnp.full((8, lanes), FLOOR, F32)
            for i in range(chunks):
                rows = pl.ds((i % (chunks // 2)) * chunk, chunk)
                s = dot_nt(kb[i // (chunks // 2), rows, head(n)], qv) * (SCALE * LOG2E)
                s = s + bias[which, pl.ds(i * chunk, chunk)]
                sbuf[pl.ds(i * chunk, chunk)] = s
                top = jnp.maximum(top, jnp.max(s.reshape(chunk // 8, 8, lanes), axis=0))
            m = jnp.max(top, axis=0, keepdims=True)
            total = jnp.zeros((8, lanes), F32)
            for i in range(chunks):
                e = jnp.exp2(sbuf[pl.ds(i * chunk, chunk)] - m)
                total = total + jnp.sum(e.reshape(chunk // 8, 8, lanes), axis=0)
                probs[u, n, pl.ds(i * chunk, chunk)] = e.astype(BF16)
            total = jnp.maximum(jnp.sum(total, axis=0, keepdims=True), 1e-37)
            put(loc, places, n, m)
            put(loc, places, 4 + n, 1.0 / total)
            put(st, places, n, m + jnp.log2(total))

    k_load.wait()
    v_load.wait()
    for cp in q_copies:
        cp.wait()
    arrived(kb.at[1 - t], sib_s.at[0], sib_r.at[0])
    arrived(vb.at[1 - t], sib_s.at[1], sib_r.at[1])
    arrived(qx.at[4, :, 1 - t], sib_s.at[2], sib_r.at[2])
    arrived(qx.at[5, :, 1 - t], sib_s.at[3], sib_r.at[3])
    for n in range(heads):
        kt[n] = jnp.transpose(kb[:, :, head(n)].reshape(nk, HD))
    for g in range(2):
        score_block(4 + g, own(g), 1)

    w_load.wait()

    def d_send(i, c, d):
        return remote(
            down.at[i, :, part(c)],
            dx.at[i, 1 - d, t],
            d_s.at[i, d, c],
            d_r.at[i, 1 - d, t],
            (c, h - 1 + 2 * d, y),
        )

    def d_sib(i):
        return remote(
            down.at[i, :, other], dx.at[4 + i // 2, i % 2, t], d_s.at[i, 2, 0], d_r.at[i, 2, 0], sib
        )

    def d_own(i):
        return pltpu.make_async_copy(down.at[i, :, mine], dx.at[4 + i // 2, i % 2, t], lsem.at[9 + i])

    def project(i, count):
        src = gall[pl.ds(i, count)].reshape(count * shard, gall.shape[2])
        d = dot_nt(src, wall[...]).astype(BF16)
        down[pl.ds(i, count)] = d.reshape(count, shard, d.shape[1])

    def d_go(i):
        both(lambda d: [d_send(i, c, d).start() for c in range(2)])
        d_sib(i).start()
        d_own(i).start()

    def d_here(i):
        d_own(i).wait()
        arrived(dx.at[4 + i // 2, i % 2, 1 - t], d_s.at[i, 2, 0], d_r.at[i, 2, 0])

    def d_near(i):
        both(
            lambda d: [arrived(dx.at[i, d, tq], d_s.at[i, d, tq], d_r.at[i, d, tq]) for tq in range(2)]
        )

    project(0, 1)
    d_go(0)
    arrived(gall.at[2, first], g_s.at[0], g_r.at[0])
    arrived(gall.at[1, second], g_s.at[1], g_r.at[1])
    for cp in g_sends:
        cp.wait_send()
    for cp in g_relays:
        cp.start()
    arrived(gall.at[1, first], g_s.at[3], g_r.at[3])
    arrived(gall.at[2, second], g_s.at[2], g_r.at[2])
    project(1, 2)
    d_go(1)

    both(lambda d: [arrived(qx.at[pl.ds(0, 4), d, tq], q_s.at[d, tq], q_r.at[d, tq]) for tq in range(2)])

    @pl.loop(0, 4)
    def _(s):
        score_block(s, halo(s), 0)

    d_go(2)

    def exchange(own, got, ssem, rsem):
        def copies():
            return (
                (up, remote(own.at[pl.ds(0, 2)], got.at[pl.ds(3, 2)], ssem.at[0], rsem.at[1], (t, h - 1, y))),
                (dn, remote(own.at[pl.ds(1, 2)], got.at[pl.ds(1, 2)], ssem.at[1], rsem.at[0], (t, h + 1, y))),
                (up2, remote(own.at[0], got.at[5], ssem.at[2], rsem.at[3], (t, h - 2, y))),
                (dn2, remote(own.at[2], got.at[0], ssem.at[3], rsem.at[2], (t, h + 2, y))),
            )

        def go():
            for cond, cp in copies():
                pl.when(cond)(cp.start)

        def finish():
            for cond, cp in copies():
                pl.when(cond)(cp.wait_send)
            for cond, dst, i in (
                (up, got.at[pl.ds(1, 2)], 0),
                (dn, got.at[pl.ds(3, 2)], 1),
                (up2, got.at[0], 2),
                (dn2, got.at[5], 3),
            ):
                pl.when(cond)(lambda dst=dst, i=i: arrived(dst, ssem.at[i], rsem.at[i]))

        return go, finish

    swaps = [exchange(st.at[s], rv.at[s], st_s.at[s], st_r.at[s]) for s in range(4)]

    def delta_block(u, s, places, cols):
        size = cols.size
        for n in range(heads):
            if size == lanes:
                d = rows_block(dx, u, n)
            else:
                d = dx[u, s % 2, :, :, head(n)].reshape(pair, HD)
            total = jnp.zeros((8, size), F32)
            for i in range(chunks):
                rows = pl.ds((i % (chunks // 2)) * chunk, chunk)
                dp = dot_nt(vb[i // (chunks // 2), rows, head(n)], d)
                krows = pl.ds(i * chunk, chunk)
                dprobs[u, n, krows, cols] = dp
                x = dp * probs[u, n, krows, cols].astype(F32)
                total = total + jnp.sum(x.reshape(chunk // 8, 8, size), axis=0)
            total = jnp.sum(total, axis=0, keepdims=True)
            scale = [loc[k, b, pl.ds(4 + n, 1)] for k, b in places]
            scale = scale[0] if len(scale) == 1 else jnp.concatenate(scale, axis=1)
            put(st, places, 4 + n, total * scale)

    def deltas(s):
        d_here(s)
        delta_block(4 + s // 2, s, ((s, 1),), pl.ds((s % 2) * pair, pair))
        d_near(s)
        delta_block(s, s, halo(s), pl.ds(0, lanes))
        swaps[s][0]()

    def combine(s):
        swaps[s][1]()
        for b in range(3):
            x = [st[s, b], rv[s, 2 * b], rv[s, 2 * b + 1]]
            lse = [v[0:4] for v in x]
            top = jnp.maximum(jnp.maximum(lse[0], lse[1]), lse[2])
            weight = [jnp.exp2(v - top) for v in lse]
            total = weight[0] + weight[1] + weight[2]
            delta = (weight[0] * x[0][4:8] + weight[1] * x[1][4:8] + weight[2] * x[2][4:8]) / total
            c = jnp.exp2(loc[s, b, pl.ds(0, 4)] - (top + jnp.log2(total)))
            both_rows = jnp.concatenate([c, delta], axis=0)
            row[s, b] = both_rows
            col[s, b] = jnp.transpose(both_rows)

    def query_block(u, places):
        for n in range(heads):
            c, delta = [
                jnp.concatenate([row[s, b, pl.ds(r, 1)] for s, b in places], axis=1) for r in (n, 4 + n)
            ]
            ds = (probs[u, n].astype(F32) * (dprobs[u, n] - delta)).astype(BF16)
            dscores[u, n] = ds
            dqt = dot(kt[n], ds) * (c * SCALE)
            dq_part[u, :, :, :, head(n)] = jnp.transpose(dqt).astype(BF16).reshape(2, 2, shard, HD)

    def key_block(u, places):
        for n in range(heads):
            c = jnp.concatenate([col[s, b, :, pl.ds(n, 1)] for s, b in places], axis=0)
            dk_acc[n] += dot(dscores[u, n], (rows_block(qx, u, n).astype(F32) * c).astype(BF16))
            dv_acc[n] += dot(probs[u, n], (rows_block(dx, u, n).astype(F32) * c).astype(BF16))

    def p_send(s, j, tq):
        return remote(
            dq_part.at[s, j, tq],
            parts.at[t, 2 - 2 * j, s],
            p_s.at[s, j, tq],
            p_r.at[s, 1 - j, t],
            (tq, h - 1 + 2 * j, y),
        )

    def p_sib(g):
        return remote(
            dq_part.at[4 + g, :, 1 - t], parts.at[t, 1, pl.ds(2 * g, 2)], p_s.at[g, 2, 0], p_r.at[g, 2, 0], sib
        )

    def p_own(g):
        return pltpu.make_async_copy(dq_part.at[4 + g, :, t], parts.at[t, 1, pl.ds(2 * g, 2)], osem.at[4 + g])

    def give_back(s):
        combine(s)
        query_block(s, halo(s))
        both(lambda j: [p_send(s, j, tq).start() for tq in range(2)])

    def give_home(g):
        query_block(4 + g, own(g))
        p_sib(g).start()
        p_own(g).start()
        key_block(4 + g, own(g))

    deltas(0)
    arrived(gall.at[3, first], g_s.at[4], g_r.at[4])
    arrived(gall.at[3, second], g_s.at[5], g_r.at[5])
    project(3, 1)
    d_go(3)
    deltas(1)
    give_back(0)
    deltas(2)
    deltas(3)
    give_back(1)
    give_home(0)

    @pl.loop(0, 2)
    def _(s):
        key_block(s, halo(s))

    give_back(2)
    give_back(3)
    give_home(1)

    @pl.loop(2, 4)
    def _(s):
        key_block(s, halo(s))

    for n in range(heads):
        dv_low[:, :, head(n)] = dv_acc[n].astype(BF16).reshape(2, tile, HD)
        dk_low[:, :, head(n)] = (dk_acc[n] * SCALE).astype(BF16).reshape(2, tile, HD)
    dv_sib = remote(dv_low.at[1 - t], dv_hbm.at[:, mine], e_s.at[0], e_r.at[0], sib)
    dk_sib = remote(dk_low.at[1 - t], dk_hbm.at[:, mine], e_s.at[1], e_r.at[1], sib)
    dv_sib.start()
    dk_sib.start()
    dv_out = pltpu.make_async_copy(dv_low.at[t], dv_hbm.at[:, mine], osem.at[0])
    dk_out = pltpu.make_async_copy(dk_low.at[t], dk_hbm.at[:, mine], osem.at[1])
    dv_out.start()
    dk_out.start()

    for g in range(2):
        p_own(g).wait()
        arrived(parts.at[1 - t, 1, pl.ds(2 * g, 2)], p_s.at[g, 2, 0], p_r.at[g, 2, 0])
    for s in range(4):
        both(
            lambda d, s=s: [arrived(parts.at[c, 2 * d, s], p_s.at[s, d, c], p_r.at[s, d, c]) for c in range(2)]
        )

    @pl.when(h == 0)
    def _():
        for c in range(2):
            zero_part(0, c).wait()

    @pl.when(h == heights - 1)
    def _():
        for c in range(2):
            zero_part(2, c).wait()

    for cp in g_relays + sib_sends:
        cp.wait_send()
    both(lambda d: [q_send(c, d).wait_send() for c in range(2)])
    for i in range(4):
        both(lambda d, i=i: [d_send(i, c, d).wait_send() for c in range(2)])
        d_sib(i).wait_send()
    for s in range(4):
        both(lambda d, s=s: [p_send(s, d, tq).wait_send() for tq in range(2)])
    for g in range(2):
        p_sib(g).wait_send()
    dv_sib.wait_send()
    dk_sib.wait_send()
    arrived(dv_hbm.at[:, other], e_s.at[0], e_r.at[0])
    arrived(dk_hbm.at[:, other], e_s.at[1], e_r.at[1])
    dv_out.wait()
    dk_out.wait()


def finish(parts, dk, dv, dq_hbm, dk_hbm, dv_hbm, buf, dk_buf, dv_buf, dq_out, sem):
    y = lax.axis_index("tensor")
    shard, half = buf.shape[4:]
    loads = [
        pltpu.make_async_copy(parts.at[:, :, pl.ds(0, 2)], buf.at[0], sem.at[0]),
        pltpu.make_async_copy(parts.at[:, :, pl.ds(2, 2)], buf.at[1], sem.at[1]),
        pltpu.make_async_copy(dk, dk_buf, sem.at[2]),
        pltpu.make_async_copy(dv, dv_buf, sem.at[3]),
    ]
    stores = [
        pltpu.make_async_copy(dk_buf, dk_hbm, sem.at[4]),
        pltpu.make_async_copy(dv_buf, dv_hbm, sem.at[5]),
    ]
    for k in range(4):
        rows = pl.ds(pl.multiple_of(lax.rem(y + SHARD[k], 4) * shard, shard), shard)
        stores.append(
            pltpu.make_async_copy(
                dq_out.at[k], dq_hbm.at[rows], sem.at[6 + k]
            )
        )
    for i in (2, 3, 0, 1):
        loads[i].start()
    for i in range(2):
        loads[2 + i].wait()
        stores[i].start()
    for g in range(2):
        loads[g].wait()
        for c in range(2):
            x = buf[g, c, 0].astype(F32) + buf[g, c, 1].astype(F32) + buf[g, c, 2].astype(F32)
            dq_out[pl.ds(2 * g, 2), :, pl.ds(c * half, half)] = x.astype(BF16)
        stores[2 + 2 * g].start()
        stores[3 + 2 * g].start()
    for cp in stores:
        cp.wait()


def local(queries, key_rows, value_rows, grad_output, out_weight, window_flags, valid_counts):
    tile, width = queries.shape[3:]
    model = grad_output.shape[-1]
    half = width // 2
    heads = half // HD
    shard = tile // 4
    pair, lanes, nk = 2 * shard, 4 * shard, 2 * tile
    heights = lax.axis_size("height")
    shape = jax.ShapeDtypeStruct((tile, width), BF16)
    parts_shape = jax.ShapeDtypeStruct((2, 3, 4, shard, half), BF16)
    any_spec = pl.BlockSpec(memory_space=pl.ANY)
    dma = pltpu.SemaphoreType.DMA
    vm = pltpu.VMEM
    outs = pl.pallas_call(
        lambda *refs: kernel(heights, *refs),
        out_shape=(parts_shape, shape, shape),
        in_specs=[any_spec] * 7,
        out_specs=(any_spec, any_spec, any_spec),
        scratch_shapes=[
            vm((2, 9, 1, heights), jnp.int32),
            vm((2, 1, heights), jnp.int32),
            vm((4, shard, width), BF16),
            vm((4, shard, width), BF16),
            vm((4, shard, model), BF16),
            vm((width, model), BF16),
            vm((6, 2, 2, shard, half), BF16),
            vm((6, 2, 2, shard, half), BF16),
            vm((2, tile, half), BF16),
            vm((2, tile, half), BF16),
            vm((heads, HD, nk), BF16),
            vm((2, nk, lanes), F32),
            vm((nk, lanes), F32),
            vm((6, heads, nk, lanes), BF16),
            vm((6, heads, nk, lanes), F32),
            vm((6, heads, nk, lanes), BF16),
            vm((heads, nk, HD), F32),
            vm((heads, nk, HD), F32),
            vm((2, tile, half), BF16),
            vm((2, tile, half), BF16),
            vm((6, 2, 2, shard, half), BF16),
            vm((4, 3, 8, pair), F32),
            vm((4, 6, 8, pair), F32),
            vm((4, 3, 8, pair), F32),
            vm((4, 3, 8, pair), F32),
            vm((4, 3, pair, 8), F32),
            dma((16,)),
            dma((6,)),
            dma((6,)),
            dma((6,)),
            dma((2, 2)),
            dma((2, 2)),
            dma((4,)),
            dma((4,)),
            dma((4, 3, 2)),
            dma((4, 3, 2)),
            dma((4, 4)),
            dma((4, 4)),
            dma((4, 3, 2)),
            dma((4, 3, 2)),
            dma((2,)),
            dma((2,)),
        ],
        compiler_params=pltpu.CompilerParams(
            collective_id=0, has_side_effects=True, vmem_limit_bytes=56 * 2**20
        ),
    )(
        window_flags.transpose(0, 3, 2, 1),
        valid_counts.transpose(0, 2, 1),
        queries.reshape(tile, width),
        key_rows.reshape(tile, width),
        value_rows.reshape(tile, width),
        grad_output.reshape(grad_output.shape[3], model),
        out_weight,
    )
    outs = pl.pallas_call(
        finish,
        out_shape=(shape, shape, shape),
        in_specs=[any_spec] * 3,
        out_specs=(any_spec,) * 3,
        scratch_shapes=[
            vm((2, 2, 3, 2, shard, half), BF16),
            vm((tile, width), BF16),
            vm((tile, width), BF16),
            vm((4, shard, width), BF16),
            dma((10,)),
        ],
    )(*outs)
    return tuple(x.reshape(queries.shape) for x in outs)


def solution(mesh):
    wide = P("tm", "height", None, None, "tensor")
    placed = (wide, wide, wide, P("tm", "height", None, "tensor", None), P("tensor", None), P(), P())
    return jax.shard_map(local, mesh=mesh, in_specs=placed, out_specs=(wide, wide, wide), check_vma=False)
```

```python
import jax
import jax.numpy as jnp
from jax import lax
from jax.experimental import pallas as pl
from jax.experimental.pallas import tpu as pltpu
from jax.sharding import PartitionSpec as P

HD = 128
SCALE = HD ** (-0.5)
LOG2E = 1.4426950408889634
MASKED = -1e30
FLOOR = -1e25
MESH = pl.DeviceIdType.MESH
F32 = jnp.float32
BF16 = jnp.bfloat16
SHARD = (0, 1, 3, 2)
NT = (((1,), (1,)), ((), ()))


def dot(a, b):
    return jnp.dot(a, b, preferred_element_type=F32)


def dot_nt(a, b):
    return lax.dot_general(a, b, NT, preferred_element_type=F32)


def kernel(
    heights,
    f_hbm,
    n_hbm,
    q_hbm,
    k_hbm,
    v_hbm,
    g_hbm,
    w_hbm,
    parts,
    dk_hbm,
    dv_hbm,
    flags,
    counts,
    qown,
    down,
    gall,
    wall,
    wt,
    qx,
    dx,
    kb,
    vb,
    kt,
    bias,
    sbuf,
    probs,
    dprobs,
    dscores,
    dk_acc,
    dv_acc,
    dk_low,
    dv_low,
    dq_part,
    st,
    rv,
    loc,
    row,
    col,
    lsem,
    osem,
    g_s,
    g_r,
    q_s,
    q_r,
    sib_s,
    sib_r,
    d_s,
    d_r,
    st_s,
    st_r,
    p_s,
    p_r,
    e_s,
    e_r,
):
    t = lax.axis_index("tm")
    h = lax.axis_index("height")
    y = lax.axis_index("tensor")
    half = k_hbm.shape[1] // 2
    heads = half // HD
    tile = k_hbm.shape[0]
    shard = tile // 4
    pair = 2 * shard
    lanes = 2 * pair
    sib = (1 - t, h, y)
    up, dn, up2, dn2 = h > 0, h < heights - 1, h > 1, h < heights - 2
    mine = pl.ds(pl.multiple_of(t * half, HD), half)
    other = pl.ds(pl.multiple_of((1 - t) * half, HD), half)

    def rows_of(k):
        return pl.ds(pl.multiple_of(lax.rem(y + SHARD[k], 4) * shard, shard), shard)

    def remote(src, dst, ssem, rsem, dev):
        return pltpu.make_async_remote_copy(
            src_ref=src, dst_ref=dst, send_sem=ssem, recv_sem=rsem, device_id=dev, device_id_type=MESH
        )

    def arrived(dst, ssem, rsem):
        remote(dst, dst, ssem, rsem, sib).wait_recv()

    def sent(src, ssem, rsem):
        remote(src, src, ssem, rsem, sib).wait_send()

    q_loads = [pltpu.make_async_copy(q_hbm.at[rows_of(k)], qown.at[k], lsem.at[k]) for k in range(4)]
    g_load = pltpu.make_async_copy(g_hbm, gall.at[0], lsem.at[4])
    k_load = pltpu.make_async_copy(k_hbm.at[:, mine], kb.at[t], lsem.at[5])
    v_load = pltpu.make_async_copy(v_hbm.at[:, mine], vb.at[t], lsem.at[6])
    w_load = pltpu.make_async_copy(w_hbm, wall, lsem.at[7])
    f_load = pltpu.make_async_copy(f_hbm, flags, lsem.at[13])
    n_load = pltpu.make_async_copy(n_hbm, counts, lsem.at[14])
    f_load.start()
    n_load.start()
    g_load.start()
    for cp in q_loads:
        cp.start()
    k_load.start()
    v_load.start()
    w_load.start()

    barrier = pltpu.get_barrier_semaphore()

    def greet(dev):
        pl.semaphore_signal(barrier, inc=1, device_id=dev, device_id_type=MESH)

    greet(sib)
    for k in (1, 2, 3):
        greet((t, h, lax.rem(y + k, 4)))

    @pl.when(up)
    def _():
        greet((0, h - 1, y))
        greet((1, h - 1, y))

    @pl.when(dn)
    def _():
        greet((0, h + 1, y))
        greet((1, h + 1, y))

    @pl.when(up2)
    def _():
        greet((t, h - 2, y))

    @pl.when(dn2)
    def _():
        greet((t, h + 2, y))

    def zero_part(b, c):
        return pltpu.make_async_copy(dx.at[pl.ds(0, 4), b // 2, c], parts.at[c, b], osem.at[2 + c])

    def absent(b):
        for k in range(4):
            qx[k, b // 2] = jnp.zeros(qx.shape[2:], BF16)
            dx[k, b // 2] = jnp.zeros(dx.shape[2:], BF16)
        for c in range(2):
            zero_part(b, c).start()

    sub = lax.broadcasted_iota(jnp.int32, (8, pair), 0)
    nothing = jnp.where(sub < 4, FLOOR, 0.0).astype(F32)
    zeros = jnp.zeros((8, pair), F32)

    def absent_stats(i):
        for k in range(4):
            rv[k, i] = nothing

    @pl.when(h == 0)
    def _():
        absent(0)
        absent_stats(1)
        absent_stats(2)

    @pl.when(h == heights - 1)
    def _():
        absent(2)
        absent_stats(3)
        absent_stats(4)

    @pl.when(h <= 1)
    def _():
        absent_stats(0)

    @pl.when(h >= heights - 2)
    def _():
        absent_stats(5)

    for k in range(4):
        for b in range(3):
            st[k, b] = zeros
            loc[k, b] = zeros
    dk_acc[...] = jnp.zeros(dk_acc.shape, F32)
    dv_acc[...] = jnp.zeros(dv_acc.shape, F32)

    f_load.wait()
    n_load.wait()
    position = lax.broadcasted_iota(jnp.int32, (tile, pair), 0).astype(F32)
    late = lax.broadcasted_iota(jnp.int32, (1, pair), 1) >= shard
    lane = lax.broadcasted_iota(jnp.int32, (1, heights), 1)

    def at_height(values, i):
        return jnp.sum(jnp.where(lane == i, values.astype(F32), 0.0), axis=1, keepdims=True)

    for b in range(3):
        hq = h + b - 1
        inside = (hq >= 0) & (hq < heights)
        hq = jnp.clip(hq, 0, heights - 1)
        for tk in range(2):
            count = []
            for tq in range(2):
                flag = at_height(flags[tq, 3 * (tk - tq + 1) + 2 - b], hq)
                count.append(jnp.where(inside & (flag > 0.0), at_height(counts[tk], h), 0.0))
            limit = jnp.where(late, count[1], count[0])
            value = jnp.where(position < limit, 0.0, MASKED).astype(F32)
            krows = pl.ds(tk * tile, tile)
            if b == 1:
                bias[1, krows, pl.ds(0, pair)] = value
                bias[1, krows, pl.ds(pair, pair)] = value
            else:
                bias[0, krows, pl.ds((b // 2) * pair, pair)] = value

    pl.semaphore_wait(
        barrier,
        4
        + 2 * up.astype(jnp.int32)
        + 2 * dn.astype(jnp.int32)
        + up2.astype(jnp.int32)
        + dn2.astype(jnp.int32),
    )

    g_load.wait()
    ahead, behind = (t, h, lax.rem(y + 1, 4)), (t, h, lax.rem(y + 3, 4))
    first, second = pl.ds(0, shard // 2), pl.ds(shard // 2, shard // 2)
    g_sends = [
        remote(gall.at[0, first], gall.at[2, first], g_s.at[0], g_r.at[0], ahead),
        remote(gall.at[0, second], gall.at[1, second], g_s.at[1], g_r.at[1], behind),
        remote(gall.at[0, second], gall.at[2, second], g_s.at[2], g_r.at[2], ahead),
        remote(gall.at[0, first], gall.at[1, first], g_s.at[3], g_r.at[3], behind),
    ]
    g_relays = [
        remote(gall.at[2, first], gall.at[3, first], g_s.at[4], g_r.at[4], ahead),
        remote(gall.at[1, second], gall.at[3, second], g_s.at[5], g_r.at[5], behind),
    ]
    for cp in g_sends:
        cp.start()
    for cp in q_loads:
        cp.wait()
    sib_sends = [
        remote(k_hbm.at[:, other], kb.at[t], sib_s.at[0], sib_r.at[0], sib),
        remote(v_hbm.at[:, other], vb.at[t], sib_s.at[1], sib_r.at[1], sib),
        remote(qown.at[pl.ds(0, 2), :, other], qx.at[4, :, t], sib_s.at[2], sib_r.at[2], sib),
        remote(qown.at[pl.ds(2, 2), :, other], qx.at[5, :, t], sib_s.at[3], sib_r.at[3], sib),
    ]
    for cp in sib_sends:
        cp.start()

    def part(c):
        return pl.ds(c * half, half)

    def q_send(c, d):
        return remote(
            qown.at[:, :, part(c)],
            qx.at[pl.ds(0, 4), 1 - d, t],
            q_s.at[d, c],
            q_r.at[1 - d, t],
            (c, h - 1 + 2 * d, y),
        )

    def both(fn):
        @pl.when(up)
        def _():
            fn(0)

        @pl.when(dn)
        def _():
            fn(1)

    both(lambda d: [q_send(c, d).start() for c in range(2)])
    q_copies = [
        pltpu.make_async_copy(qown.at[pl.ds(2 * g, 2), :, mine], qx.at[4 + g, :, t], lsem.at[(8, 15)[g]])
        for g in range(2)
    ]
    for cp in q_copies:
        cp.start()

    chunk = 256
    nk = 2 * tile
    chunks = nk // chunk

    def head(n):
        return pl.ds(n * HD, HD)

    def rows_block(ref, u, n):
        return ref[u, :, :, :, head(n)].reshape(lanes, HD)

    def halo(s):
        return ((s, 0), (s, 2))

    def own(g):
        return ((2 * g, 1), (2 * g + 1, 1))

    def put(ref, places, r, value):
        for i, (s, b) in enumerate(places):
            ref[s, b, pl.ds(r, 1)] = value[:, i * pair : (i + 1) * pair]

    def score_block(u, places, which):
        for n in range(heads):
            qv = rows_block(qx, u, n)
            top = jnp.full((8, lanes), FLOOR, F32)
            for i in range(chunks):
                rows = pl.ds((i % (chunks // 2)) * chunk, chunk)
                s = dot_nt(kb[i // (chunks // 2), rows, head(n)], qv) * (SCALE * LOG2E)
                s = s + bias[which, pl.ds(i * chunk, chunk)]
                sbuf[pl.ds(i * chunk, chunk)] = s
                top = jnp.maximum(top, jnp.max(s.reshape(chunk // 8, 8, lanes), axis=0))
            m = jnp.max(top, axis=0, keepdims=True)
            total = jnp.zeros((8, lanes), F32)
            for i in range(chunks):
                e = jnp.exp2(sbuf[pl.ds(i * chunk, chunk)] - m)
                total = total + jnp.sum(e.reshape(chunk // 8, 8, lanes), axis=0)
                probs[u, n, pl.ds(i * chunk, chunk)] = e.astype(BF16)
            total = jnp.maximum(jnp.sum(total, axis=0, keepdims=True), 1e-37)
            put(loc, places, n, m)
            put(loc, places, 4 + n, 1.0 / total)
            put(st, places, n, m + jnp.log2(total))

    k_load.wait()
    v_load.wait()
    for cp in q_copies:
        cp.wait()
    arrived(kb.at[1 - t], sib_s.at[0], sib_r.at[0])
    arrived(vb.at[1 - t], sib_s.at[1], sib_r.at[1])
    arrived(qx.at[4, :, 1 - t], sib_s.at[2], sib_r.at[2])
    arrived(qx.at[5, :, 1 - t], sib_s.at[3], sib_r.at[3])
    for n in range(heads):
        kt[n] = jnp.transpose(kb[:, :, head(n)].reshape(nk, HD))
    for g in range(2):
        score_block(4 + g, own(g), 1)

    w_load.wait()
    for i in range(0, wt.shape[0], 512):
        wt[pl.ds(i, 512)] = jnp.transpose(wall[:, pl.ds(i, 512)])

    def d_send(i, c, d):
        return remote(
            down.at[i, :, part(c)],
            dx.at[i, 1 - d, t],
            d_s.at[i, d, c],
            d_r.at[i, 1 - d, t],
            (c, h - 1 + 2 * d, y),
        )

    def d_sib(i):
        return remote(
            down.at[i, :, other], dx.at[4 + i // 2, i % 2, t], d_s.at[i, 2, 0], d_r.at[i, 2, 0], sib
        )

    def d_own(i):
        return pltpu.make_async_copy(down.at[i, :, mine], dx.at[4 + i // 2, i % 2, t], lsem.at[9 + i])

    def project(i, count):
        src = gall[pl.ds(i, count)].reshape(count * shard, gall.shape[2])
        d = dot(src, wt[...]).astype(BF16)
        down[pl.ds(i, count)] = d.reshape(count, shard, d.shape[1])

    def d_go(i):
        both(lambda d: [d_send(i, c, d).start() for c in range(2)])
        d_sib(i).start()
        d_own(i).start()

    def d_here(i):
        d_own(i).wait()
        arrived(dx.at[4 + i // 2, i % 2, 1 - t], d_s.at[i, 2, 0], d_r.at[i, 2, 0])

    def d_near(i):
        both(
            lambda d: [arrived(dx.at[i, d, tq], d_s.at[i, d, tq], d_r.at[i, d, tq]) for tq in range(2)]
        )

    project(0, 1)
    d_go(0)
    arrived(gall.at[2, first], g_s.at[0], g_r.at[0])
    arrived(gall.at[1, second], g_s.at[1], g_r.at[1])
    for cp in g_sends:
        cp.wait_send()
    for cp in g_relays:
        cp.start()
    arrived(gall.at[1, first], g_s.at[3], g_r.at[3])
    arrived(gall.at[2, second], g_s.at[2], g_r.at[2])
    project(1, 2)
    d_go(1)

    both(lambda d: [arrived(qx.at[pl.ds(0, 4), d, tq], q_s.at[d, tq], q_r.at[d, tq]) for tq in range(2)])

    @pl.loop(0, 4)
    def _(s):
        score_block(s, halo(s), 0)

    d_go(2)

    def exchange(own, got, ssem, rsem):
        def copies():
            return (
                (up, remote(own.at[pl.ds(0, 2)], got.at[pl.ds(3, 2)], ssem.at[0], rsem.at[1], (t, h - 1, y))),
                (dn, remote(own.at[pl.ds(1, 2)], got.at[pl.ds(1, 2)], ssem.at[1], rsem.at[0], (t, h + 1, y))),
                (up2, remote(own.at[0], got.at[5], ssem.at[2], rsem.at[3], (t, h - 2, y))),
                (dn2, remote(own.at[2], got.at[0], ssem.at[3], rsem.at[2], (t, h + 2, y))),
            )

        def go():
            for cond, cp in copies():
                pl.when(cond)(cp.start)

        def finish():
            for cond, cp in copies():
                pl.when(cond)(cp.wait_send)
            for cond, dst, i in (
                (up, got.at[pl.ds(1, 2)], 0),
                (dn, got.at[pl.ds(3, 2)], 1),
                (up2, got.at[0], 2),
                (dn2, got.at[5], 3),
            ):
                pl.when(cond)(lambda dst=dst, i=i: arrived(dst, ssem.at[i], rsem.at[i]))

        return go, finish

    swaps = [exchange(st.at[s], rv.at[s], st_s.at[s], st_r.at[s]) for s in range(4)]

    def delta_block(u, s, places, cols):
        size = cols.size
        for n in range(heads):
            if size == lanes:
                d = rows_block(dx, u, n)
            else:
                d = dx[u, s % 2, :, :, head(n)].reshape(pair, HD)
            total = jnp.zeros((8, size), F32)
            for i in range(chunks):
                rows = pl.ds((i % (chunks // 2)) * chunk, chunk)
                dp = dot_nt(vb[i // (chunks // 2), rows, head(n)], d)
                krows = pl.ds(i * chunk, chunk)
                dprobs[u, n, krows, cols] = dp
                x = dp * probs[u, n, krows, cols].astype(F32)
                total = total + jnp.sum(x.reshape(chunk // 8, 8, size), axis=0)
            total = jnp.sum(total, axis=0, keepdims=True)
            scale = [loc[k, b, pl.ds(4 + n, 1)] for k, b in places]
            scale = scale[0] if len(scale) == 1 else jnp.concatenate(scale, axis=1)
            put(st, places, 4 + n, total * scale)

    def deltas(s):
        d_here(s)
        delta_block(4 + s // 2, s, ((s, 1),), pl.ds((s % 2) * pair, pair))
        d_near(s)
        delta_block(s, s, halo(s), pl.ds(0, lanes))
        swaps[s][0]()

    def combine(s):
        swaps[s][1]()
        for b in range(3):
            x = [st[s, b], rv[s, 2 * b], rv[s, 2 * b + 1]]
            lse = [v[0:4] for v in x]
            top = jnp.maximum(jnp.maximum(lse[0], lse[1]), lse[2])
            weight = [jnp.exp2(v - top) for v in lse]
            total = weight[0] + weight[1] + weight[2]
            delta = (weight[0] * x[0][4:8] + weight[1] * x[1][4:8] + weight[2] * x[2][4:8]) / total
            c = jnp.exp2(loc[s, b, pl.ds(0, 4)] - (top + jnp.log2(total)))
            both_rows = jnp.concatenate([c, delta], axis=0)
            row[s, b] = both_rows
            col[s, b] = jnp.transpose(both_rows)

    def query_block(u, places):
        for n in range(heads):
            c, delta = [
                jnp.concatenate([row[s, b, pl.ds(r, 1)] for s, b in places], axis=1) for r in (n, 4 + n)
            ]
            ds = (probs[u, n].astype(F32) * (dprobs[u, n] - delta)).astype(BF16)
            dscores[u, n] = ds
            dqt = dot(kt[n], ds) * (c * SCALE)
            dq_part[u, :, :, :, head(n)] = jnp.transpose(dqt).astype(BF16).reshape(2, 2, shard, HD)

    def key_block(u, places):
        for n in range(heads):
            c = jnp.concatenate([col[s, b, :, pl.ds(n, 1)] for s, b in places], axis=0)
            dk_acc[n] += dot(dscores[u, n], (rows_block(qx, u, n).astype(F32) * c).astype(BF16))
            dv_acc[n] += dot(probs[u, n], (rows_block(dx, u, n).astype(F32) * c).astype(BF16))

    def p_send(s, j, tq):
        return remote(
            dq_part.at[s, j, tq],
            parts.at[t, 2 - 2 * j, s],
            p_s.at[s, j, tq],
            p_r.at[s, 1 - j, t],
            (tq, h - 1 + 2 * j, y),
        )

    def p_sib(g):
        return remote(
            dq_part.at[4 + g, :, 1 - t], parts.at[t, 1, pl.ds(2 * g, 2)], p_s.at[g, 2, 0], p_r.at[g, 2, 0], sib
        )

    def p_own(g):
        return pltpu.make_async_copy(dq_part.at[4 + g, :, t], parts.at[t, 1, pl.ds(2 * g, 2)], osem.at[4 + g])

    def give_back(s):
        combine(s)
        query_block(s, halo(s))
        both(lambda j: [p_send(s, j, tq).start() for tq in range(2)])

    def give_home(g):
        query_block(4 + g, own(g))
        p_sib(g).start()
        p_own(g).start()

    deltas(0)
    arrived(gall.at[3, first], g_s.at[4], g_r.at[4])
    arrived(gall.at[3, second], g_s.at[5], g_r.at[5])
    project(3, 1)
    d_go(3)
    deltas(1)
    give_back(0)
    deltas(2)
    key_block(0, halo(0))
    deltas(3)
    give_back(1)
    key_block(1, halo(1))
    give_home(0)
    key_block(4, own(0))
    give_back(2)
    key_block(2, halo(2))
    give_back(3)
    give_home(1)
    key_block(5, own(1))
    key_block(3, halo(3))

    for n in range(heads):
        dv_low[:, :, head(n)] = dv_acc[n].astype(BF16).reshape(2, tile, HD)
        dk_low[:, :, head(n)] = (dk_acc[n] * SCALE).astype(BF16).reshape(2, tile, HD)
    dv_sib = remote(dv_low.at[1 - t], dv_hbm.at[:, mine], e_s.at[0], e_r.at[0], sib)
    dk_sib = remote(dk_low.at[1 - t], dk_hbm.at[:, mine], e_s.at[1], e_r.at[1], sib)
    dv_sib.start()
    dk_sib.start()
    dv_out = pltpu.make_async_copy(dv_low.at[t], dv_hbm.at[:, mine], osem.at[0])
    dk_out = pltpu.make_async_copy(dk_low.at[t], dk_hbm.at[:, mine], osem.at[1])
    dv_out.start()
    dk_out.start()

    for g in range(2):
        p_own(g).wait()
        arrived(parts.at[1 - t, 1, pl.ds(2 * g, 2)], p_s.at[g, 2, 0], p_r.at[g, 2, 0])
    for s in range(4):
        both(
            lambda d, s=s: [arrived(parts.at[c, 2 * d, s], p_s.at[s, d, c], p_r.at[s, d, c]) for c in range(2)]
        )

    @pl.when(h == 0)
    def _():
        for c in range(2):
            zero_part(0, c).wait()

    @pl.when(h == heights - 1)
    def _():
        for c in range(2):
            zero_part(2, c).wait()

    for cp in g_relays + sib_sends:
        cp.wait_send()
    both(lambda d: [q_send(c, d).wait_send() for c in range(2)])
    for i in range(4):
        both(lambda d, i=i: [d_send(i, c, d).wait_send() for c in range(2)])
        d_sib(i).wait_send()
    for s in range(4):
        both(lambda d, s=s: [p_send(s, d, tq).wait_send() for tq in range(2)])
    for g in range(2):
        p_sib(g).wait_send()
    dv_sib.wait_send()
    dk_sib.wait_send()
    arrived(dv_hbm.at[:, other], e_s.at[0], e_r.at[0])
    arrived(dk_hbm.at[:, other], e_s.at[1], e_r.at[1])
    dv_out.wait()
    dk_out.wait()


def finish(parts, dk, dv, dq_hbm, dk_hbm, dv_hbm, buf, dk_buf, dv_buf, dq_out, sem):
    y = lax.axis_index("tensor")
    shard, half = buf.shape[4:]
    loads = [
        pltpu.make_async_copy(parts.at[:, :, pl.ds(0, 2)], buf.at[0], sem.at[0]),
        pltpu.make_async_copy(parts.at[:, :, pl.ds(2, 2)], buf.at[1], sem.at[1]),
        pltpu.make_async_copy(dk, dk_buf, sem.at[2]),
        pltpu.make_async_copy(dv, dv_buf, sem.at[3]),
    ]
    stores = [
        pltpu.make_async_copy(dk_buf, dk_hbm, sem.at[4]),
        pltpu.make_async_copy(dv_buf, dv_hbm, sem.at[5]),
    ]
    for k in range(4):
        rows = pl.ds(pl.multiple_of(lax.rem(y + SHARD[k], 4) * shard, shard), shard)
        stores.append(
            pltpu.make_async_copy(
                dq_out.at[k], dq_hbm.at[rows], sem.at[6 + k]
            )
        )
    for i in (2, 3, 0, 1):
        loads[i].start()
    for i in range(2):
        loads[2 + i].wait()
        stores[i].start()
    for g in range(2):
        loads[g].wait()
        for c in range(2):
            x = buf[g, c, 0].astype(F32) + buf[g, c, 1].astype(F32) + buf[g, c, 2].astype(F32)
            dq_out[pl.ds(2 * g, 2), :, pl.ds(c * half, half)] = x.astype(BF16)
        stores[2 + 2 * g].start()
        stores[3 + 2 * g].start()
    for cp in stores:
        cp.wait()


def local(queries, key_rows, value_rows, grad_output, out_weight, window_flags, valid_counts):
    tile, width = queries.shape[3:]
    model = grad_output.shape[-1]
    half = width // 2
    heads = half // HD
    shard = tile // 4
    pair, lanes, nk = 2 * shard, 4 * shard, 2 * tile
    heights = lax.axis_size("height")
    shape = jax.ShapeDtypeStruct((tile, width), BF16)
    parts_shape = jax.ShapeDtypeStruct((2, 3, 4, shard, half), BF16)
    any_spec = pl.BlockSpec(memory_space=pl.ANY)
    dma = pltpu.SemaphoreType.DMA
    vm = pltpu.VMEM
    outs = pl.pallas_call(
        lambda *refs: kernel(heights, *refs),
        out_shape=(parts_shape, shape, shape),
        in_specs=[any_spec] * 7,
        out_specs=(any_spec, any_spec, any_spec),
        scratch_shapes=[
            vm((2, 9, 1, heights), jnp.int32),
            vm((2, 1, heights), jnp.int32),
            vm((4, shard, width), BF16),
            vm((4, shard, width), BF16),
            vm((4, shard, model), BF16),
            vm((width, model), BF16),
            vm((model, width), BF16),
            vm((6, 2, 2, shard, half), BF16),
            vm((6, 2, 2, shard, half), BF16),
            vm((2, tile, half), BF16),
            vm((2, tile, half), BF16),
            vm((heads, HD, nk), BF16),
            vm((2, nk, lanes), F32),
            vm((nk, lanes), F32),
            vm((6, heads, nk, lanes), BF16),
            vm((6, heads, nk, lanes), F32),
            vm((6, heads, nk, lanes), BF16),
            vm((heads, nk, HD), F32),
            vm((heads, nk, HD), F32),
            vm((2, tile, half), BF16),
            vm((2, tile, half), BF16),
            vm((6, 2, 2, shard, half), BF16),
            vm((4, 3, 8, pair), F32),
            vm((4, 6, 8, pair), F32),
            vm((4, 3, 8, pair), F32),
            vm((4, 3, 8, pair), F32),
            vm((4, 3, pair, 8), F32),
            dma((16,)),
            dma((6,)),
            dma((6,)),
            dma((6,)),
            dma((2, 2)),
            dma((2, 2)),
            dma((4,)),
            dma((4,)),
            dma((4, 3, 2)),
            dma((4, 3, 2)),
            dma((4, 4)),
            dma((4, 4)),
            dma((4, 3, 2)),
            dma((4, 3, 2)),
            dma((2,)),
            dma((2,)),
        ],
        compiler_params=pltpu.CompilerParams(
            collective_id=0, has_side_effects=True, vmem_limit_bytes=56 * 2**20
        ),
    )(
        window_flags.transpose(0, 3, 2, 1),
        valid_counts.transpose(0, 2, 1),
        queries.reshape(tile, width),
        key_rows.reshape(tile, width),
        value_rows.reshape(tile, width),
        grad_output.reshape(grad_output.shape[3], model),
        out_weight,
    )
    outs = pl.pallas_call(
        finish,
        out_shape=(shape, shape, shape),
        in_specs=[any_spec] * 3,
        out_specs=(any_spec,) * 3,
        scratch_shapes=[
            vm((2, 2, 3, 2, shard, half), BF16),
            vm((tile, width), BF16),
            vm((tile, width), BF16),
            vm((4, shard, width), BF16),
            dma((10,)),
        ],
    )(*outs)
    return tuple(x.reshape(queries.shape) for x in outs)


def solution(mesh):
    wide = P("tm", "height", None, None, "tensor")
    placed = (wide, wide, wide, P("tm", "height", None, "tensor", None), P("tensor", None), P(), P())
    return jax.shard_map(local, mesh=mesh, in_specs=placed, out_specs=(wide, wide, wide), check_vma=False)
```

```python
import jax
import jax.numpy as jnp
from jax import lax
from jax.experimental import pallas as pl
from jax.experimental.pallas import tpu as pltpu
from jax.sharding import PartitionSpec as P

HD = 128
SCALE = HD ** (-0.5)
LOG2E = 1.4426950408889634
MASKED = -1e30
FLOOR = -1e25
MESH = pl.DeviceIdType.MESH
F32 = jnp.float32
BF16 = jnp.bfloat16
SHARD = (0, 1, 3, 2)
NT = (((1,), (1,)), ((), ()))


def dot(a, b):
    return jnp.dot(a, b, preferred_element_type=F32)


def dot_nt(a, b):
    return lax.dot_general(a, b, NT, preferred_element_type=F32)


def kernel(
    heights,
    f_hbm,
    n_hbm,
    q_hbm,
    k_hbm,
    v_hbm,
    g_hbm,
    w_hbm,
    parts,
    dk_hbm,
    dv_hbm,
    flags,
    counts,
    qown,
    down,
    gall,
    wall,
    wt,
    qx,
    dx,
    kb,
    vb,
    kt,
    bias,
    sbuf,
    probs,
    dprobs,
    dscores,
    dk_acc,
    dv_acc,
    dk_low,
    dv_low,
    dq_part,
    st,
    rv,
    loc,
    row,
    col,
    lsem,
    osem,
    g_s,
    g_r,
    q_s,
    q_r,
    sib_s,
    sib_r,
    d_s,
    d_r,
    st_s,
    st_r,
    p_s,
    p_r,
    e_s,
    e_r,
):
    t = lax.axis_index("tm")
    h = lax.axis_index("height")
    y = lax.axis_index("tensor")
    half = k_hbm.shape[1] // 2
    heads = half // HD
    tile = k_hbm.shape[0]
    shard = tile // 4
    pair = 2 * shard
    lanes = 2 * pair
    sib = (1 - t, h, y)
    up, dn, up2, dn2 = h > 0, h < heights - 1, h > 1, h < heights - 2
    mine = pl.ds(pl.multiple_of(t * half, HD), half)
    other = pl.ds(pl.multiple_of((1 - t) * half, HD), half)

    def rows_of(k):
        return pl.ds(pl.multiple_of(lax.rem(y + SHARD[k], 4) * shard, shard), shard)

    def remote(src, dst, ssem, rsem, dev):
        return pltpu.make_async_remote_copy(
            src_ref=src, dst_ref=dst, send_sem=ssem, recv_sem=rsem, device_id=dev, device_id_type=MESH
        )

    def arrived(dst, ssem, rsem):
        remote(dst, dst, ssem, rsem, sib).wait_recv()

    def sent(src, ssem, rsem):
        remote(src, src, ssem, rsem, sib).wait_send()

    q_loads = [pltpu.make_async_copy(q_hbm.at[rows_of(k)], qown.at[k], lsem.at[k]) for k in range(4)]
    g_load = pltpu.make_async_copy(g_hbm, gall.at[0], lsem.at[4])
    k_load = pltpu.make_async_copy(k_hbm.at[:, mine], kb.at[t], lsem.at[5])
    v_load = pltpu.make_async_copy(v_hbm.at[:, mine], vb.at[t], lsem.at[6])
    w_load = pltpu.make_async_copy(w_hbm, wall, lsem.at[7])
    f_load = pltpu.make_async_copy(f_hbm, flags, lsem.at[13])
    n_load = pltpu.make_async_copy(n_hbm, counts, lsem.at[14])
    f_load.start()
    n_load.start()
    g_load.start()
    for cp in q_loads:
        cp.start()
    k_load.start()
    v_load.start()
    w_load.start()

    barrier = pltpu.get_barrier_semaphore()

    def greet(dev):
        pl.semaphore_signal(barrier, inc=1, device_id=dev, device_id_type=MESH)

    greet(sib)
    for k in (1, 2, 3):
        greet((t, h, lax.rem(y + k, 4)))

    @pl.when(up)
    def _():
        greet((0, h - 1, y))
        greet((1, h - 1, y))

    @pl.when(dn)
    def _():
        greet((0, h + 1, y))
        greet((1, h + 1, y))

    @pl.when(up2)
    def _():
        greet((t, h - 2, y))

    @pl.when(dn2)
    def _():
        greet((t, h + 2, y))

    pl.semaphore_wait(
        barrier,
        4
        + 2 * up.astype(jnp.int32)
        + 2 * dn.astype(jnp.int32)
        + up2.astype(jnp.int32)
        + dn2.astype(jnp.int32),
    )

    ahead, behind = (t, h, lax.rem(y + 1, 4)), (t, h, lax.rem(y + 3, 4))
    first, second = pl.ds(0, shard // 2), pl.ds(shard // 2, shard // 2)
    g_sends = [
        remote(g_hbm.at[first], gall.at[2, first], g_s.at[0], g_r.at[0], ahead),
        remote(g_hbm.at[second], gall.at[1, second], g_s.at[1], g_r.at[1], behind),
        remote(g_hbm.at[second], gall.at[2, second], g_s.at[2], g_r.at[2], ahead),
        remote(g_hbm.at[first], gall.at[1, first], g_s.at[3], g_r.at[3], behind),
    ]
    g_relays = [
        remote(gall.at[2, first], gall.at[3, first], g_s.at[4], g_r.at[4], ahead),
        remote(gall.at[1, second], gall.at[3, second], g_s.at[5], g_r.at[5], behind),
    ]
    for cp in g_sends:
        cp.start()
    for cp in q_loads:
        cp.wait()
    def part(c):
        return pl.ds(c * half, half)

    def q_send(c, d):
        return remote(
            qown.at[:, :, part(c)],
            qx.at[pl.ds(0, 4), 1 - d, t],
            q_s.at[d, c],
            q_r.at[1 - d, t],
            (c, h - 1 + 2 * d, y),
        )

    def both(fn):
        @pl.when(up)
        def _():
            fn(0)

        @pl.when(dn)
        def _():
            fn(1)

    both(lambda d: [q_send(c, d).start() for c in range(2)])
    sib_sends = [
        remote(k_hbm.at[:, other], kb.at[t], sib_s.at[0], sib_r.at[0], sib),
        remote(v_hbm.at[:, other], vb.at[t], sib_s.at[1], sib_r.at[1], sib),
        remote(qown.at[pl.ds(0, 2), :, other], qx.at[4, :, t], sib_s.at[2], sib_r.at[2], sib),
        remote(qown.at[pl.ds(2, 2), :, other], qx.at[5, :, t], sib_s.at[3], sib_r.at[3], sib),
    ]
    for cp in sib_sends:
        cp.start()

    q_copies = [
        pltpu.make_async_copy(qown.at[pl.ds(2 * g, 2), :, mine], qx.at[4 + g, :, t], lsem.at[(8, 15)[g]])
        for g in range(2)
    ]
    for cp in q_copies:
        cp.start()

    def zero_part(b, c):
        return pltpu.make_async_copy(dx.at[pl.ds(0, 4), b // 2, c], parts.at[c, b], osem.at[2 + c])

    def absent(b):
        for k in range(4):
            qx[k, b // 2] = jnp.zeros(qx.shape[2:], BF16)
            dx[k, b // 2] = jnp.zeros(dx.shape[2:], BF16)
        for c in range(2):
            zero_part(b, c).start()

    sub = lax.broadcasted_iota(jnp.int32, (8, pair), 0)
    nothing = jnp.where(sub < 4, FLOOR, 0.0).astype(F32)
    zeros = jnp.zeros((8, pair), F32)

    def absent_stats(i):
        for k in range(4):
            rv[k, i] = nothing

    @pl.when(h == 0)
    def _():
        absent(0)
        absent_stats(1)
        absent_stats(2)

    @pl.when(h == heights - 1)
    def _():
        absent(2)
        absent_stats(3)
        absent_stats(4)

    @pl.when(h <= 1)
    def _():
        absent_stats(0)

    @pl.when(h >= heights - 2)
    def _():
        absent_stats(5)

    for k in range(4):
        for b in range(3):
            st[k, b] = zeros
            loc[k, b] = zeros
    dk_acc[...] = jnp.zeros(dk_acc.shape, F32)
    dv_acc[...] = jnp.zeros(dv_acc.shape, F32)

    f_load.wait()
    n_load.wait()
    position = lax.broadcasted_iota(jnp.int32, (tile, pair), 0).astype(F32)
    late = lax.broadcasted_iota(jnp.int32, (1, pair), 1) >= shard
    lane = lax.broadcasted_iota(jnp.int32, (1, heights), 1)

    def at_height(values, i):
        return jnp.sum(jnp.where(lane == i, values.astype(F32), 0.0), axis=1, keepdims=True)

    for b in range(3):
        hq = h + b - 1
        inside = (hq >= 0) & (hq < heights)
        hq = jnp.clip(hq, 0, heights - 1)
        for tk in range(2):
            count = []
            for tq in range(2):
                flag = at_height(flags[tq, 3 * (tk - tq + 1) + 2 - b], hq)
                count.append(jnp.where(inside & (flag > 0.0), at_height(counts[tk], h), 0.0))
            limit = jnp.where(late, count[1], count[0])
            value = jnp.where(position < limit, 0.0, MASKED).astype(F32)
            krows = pl.ds(tk * tile, tile)
            if b == 1:
                bias[1, krows, pl.ds(0, pair)] = value
                bias[1, krows, pl.ds(pair, pair)] = value
            else:
                bias[0, krows, pl.ds((b // 2) * pair, pair)] = value

    chunk = 256
    nk = 2 * tile
    chunks = nk // chunk

    def head(n):
        return pl.ds(n * HD, HD)

    def rows_block(ref, u, n):
        return ref[u, :, :, :, head(n)].reshape(lanes, HD)

    def halo(s):
        return ((s, 0), (s, 2))

    def own(g):
        return ((2 * g, 1), (2 * g + 1, 1))

    def put(ref, places, r, value):
        for i, (s, b) in enumerate(places):
            ref[s, b, pl.ds(r, 1)] = value[:, i * pair : (i + 1) * pair]

    def score_block(u, places, which):
        for n in range(heads):
            qv = rows_block(qx, u, n)
            top = jnp.full((8, lanes), FLOOR, F32)
            for i in range(chunks):
                rows = pl.ds((i % (chunks // 2)) * chunk, chunk)
                s = dot_nt(kb[i // (chunks // 2), rows, head(n)], qv) * (SCALE * LOG2E)
                s = s + bias[which, pl.ds(i * chunk, chunk)]
                sbuf[pl.ds(i * chunk, chunk)] = s
                top = jnp.maximum(top, jnp.max(s.reshape(chunk // 8, 8, lanes), axis=0))
            m = jnp.max(top, axis=0, keepdims=True)
            total = jnp.zeros((8, lanes), F32)
            for i in range(chunks):
                e = jnp.exp2(sbuf[pl.ds(i * chunk, chunk)] - m)
                total = total + jnp.sum(e.reshape(chunk // 8, 8, lanes), axis=0)
                probs[u, n, pl.ds(i * chunk, chunk)] = e.astype(BF16)
            total = jnp.maximum(jnp.sum(total, axis=0, keepdims=True), 1e-37)
            put(loc, places, n, m)
            put(loc, places, 4 + n, 1.0 / total)
            put(st, places, n, m + jnp.log2(total))

    k_load.wait()
    v_load.wait()
    for cp in q_copies:
        cp.wait()
    arrived(kb.at[1 - t], sib_s.at[0], sib_r.at[0])
    arrived(vb.at[1 - t], sib_s.at[1], sib_r.at[1])
    arrived(qx.at[4, :, 1 - t], sib_s.at[2], sib_r.at[2])
    arrived(qx.at[5, :, 1 - t], sib_s.at[3], sib_r.at[3])
    for n in range(heads):
        kt[n] = jnp.transpose(kb[:, :, head(n)].reshape(nk, HD))
    for g in range(2):
        score_block(4 + g, own(g), 1)

    w_load.wait()
    for i in range(0, wt.shape[0], 512):
        wt[pl.ds(i, 512)] = jnp.transpose(wall[:, pl.ds(i, 512)])

    def d_send(i, c, d):
        return remote(
            down.at[i, :, part(c)],
            dx.at[i, 1 - d, t],
            d_s.at[i, d, c],
            d_r.at[i, 1 - d, t],
            (c, h - 1 + 2 * d, y),
        )

    def d_sib(i):
        return remote(
            down.at[i, :, other], dx.at[4 + i // 2, i % 2, t], d_s.at[i, 2, 0], d_r.at[i, 2, 0], sib
        )

    def d_own(i):
        return pltpu.make_async_copy(down.at[i, :, mine], dx.at[4 + i // 2, i % 2, t], lsem.at[9 + i])

    def project(i, count):
        src = gall[pl.ds(i, count)].reshape(count * shard, gall.shape[2])
        d = dot(src, wt[...]).astype(BF16)
        down[pl.ds(i, count)] = d.reshape(count, shard, d.shape[1])

    def d_go(i):
        both(lambda d: [d_send(i, c, d).start() for c in range(2)])
        d_sib(i).start()
        d_own(i).start()

    def project_far():
        for c in range(2):
            down[3, :, part(c)] = dot(gall[3], wt[:, part(c)]).astype(BF16)
            both(lambda d, c=c: d_send(3, c, d).start())
        d_sib(3).start()
        d_own(3).start()

    def d_here(i):
        d_own(i).wait()
        arrived(dx.at[4 + i // 2, i % 2, 1 - t], d_s.at[i, 2, 0], d_r.at[i, 2, 0])

    def d_near(i):
        both(
            lambda d: [arrived(dx.at[i, d, tq], d_s.at[i, d, tq], d_r.at[i, d, tq]) for tq in range(2)]
        )

    g_load.wait()
    project(0, 1)
    d_go(0)
    arrived(gall.at[2, first], g_s.at[0], g_r.at[0])
    arrived(gall.at[1, second], g_s.at[1], g_r.at[1])
    for cp in g_sends:
        cp.wait_send()
    for cp in g_relays:
        cp.start()
    arrived(gall.at[1, first], g_s.at[3], g_r.at[3])
    arrived(gall.at[2, second], g_s.at[2], g_r.at[2])
    project(1, 2)
    d_go(1)
    d_go(2)

    both(lambda d: [arrived(qx.at[pl.ds(0, 4), d, tq], q_s.at[d, tq], q_r.at[d, tq]) for tq in range(2)])

    @pl.loop(0, 4)
    def _(s):
        score_block(s, halo(s), 0)


    def exchange(own, got, ssem, rsem):
        def copies():
            return (
                (up, remote(own.at[pl.ds(0, 2)], got.at[pl.ds(3, 2)], ssem.at[0], rsem.at[1], (t, h - 1, y))),
                (dn, remote(own.at[pl.ds(1, 2)], got.at[pl.ds(1, 2)], ssem.at[1], rsem.at[0], (t, h + 1, y))),
                (up2, remote(own.at[0], got.at[5], ssem.at[2], rsem.at[3], (t, h - 2, y))),
                (dn2, remote(own.at[2], got.at[0], ssem.at[3], rsem.at[2], (t, h + 2, y))),
            )

        def go():
            for cond, cp in copies():
                pl.when(cond)(cp.start)

        def finish():
            for cond, cp in copies():
                pl.when(cond)(cp.wait_send)
            for cond, dst, i in (
                (up, got.at[pl.ds(1, 2)], 0),
                (dn, got.at[pl.ds(3, 2)], 1),
                (up2, got.at[0], 2),
                (dn2, got.at[5], 3),
            ):
                pl.when(cond)(lambda dst=dst, i=i: arrived(dst, ssem.at[i], rsem.at[i]))

        return go, finish

    swaps = [exchange(st.at[s], rv.at[s], st_s.at[s], st_r.at[s]) for s in range(4)]

    def delta_block(u, s, places, cols):
        size = cols.size
        for n in range(heads):
            if size == lanes:
                d = rows_block(dx, u, n)
            else:
                d = dx[u, s % 2, :, :, head(n)].reshape(pair, HD)
            total = jnp.zeros((8, size), F32)
            for i in range(chunks):
                rows = pl.ds((i % (chunks // 2)) * chunk, chunk)
                dp = dot_nt(vb[i // (chunks // 2), rows, head(n)], d)
                krows = pl.ds(i * chunk, chunk)
                dprobs[u, n, krows, cols] = dp
                x = dp * probs[u, n, krows, cols].astype(F32)
                total = total + jnp.sum(x.reshape(chunk // 8, 8, size), axis=0)
            total = jnp.sum(total, axis=0, keepdims=True)
            scale = [loc[k, b, pl.ds(4 + n, 1)] for k, b in places]
            scale = scale[0] if len(scale) == 1 else jnp.concatenate(scale, axis=1)
            put(st, places, 4 + n, total * scale)

    def deltas(s):
        d_here(s)
        delta_block(4 + s // 2, s, ((s, 1),), pl.ds((s % 2) * pair, pair))
        d_near(s)
        delta_block(s, s, halo(s), pl.ds(0, lanes))
        swaps[s][0]()

    def combine(s):
        swaps[s][1]()
        for b in range(3):
            x = [st[s, b], rv[s, 2 * b], rv[s, 2 * b + 1]]
            lse = [v[0:4] for v in x]
            top = jnp.maximum(jnp.maximum(lse[0], lse[1]), lse[2])
            weight = [jnp.exp2(v - top) for v in lse]
            total = weight[0] + weight[1] + weight[2]
            delta = (weight[0] * x[0][4:8] + weight[1] * x[1][4:8] + weight[2] * x[2][4:8]) / total
            c = jnp.exp2(loc[s, b, pl.ds(0, 4)] - (top + jnp.log2(total)))
            row[s, b] = jnp.concatenate([c, delta], axis=0)

    def query_block(u, places):
        for n in range(heads):
            c, delta = [
                jnp.concatenate([row[s, b, pl.ds(r, 1)] for s, b in places], axis=1) for r in (n, 4 + n)
            ]
            ds = (probs[u, n].astype(F32) * (dprobs[u, n] - delta)).astype(BF16)
            dscores[u, n] = ds
            dqt = dot(kt[n], ds) * (c * SCALE)
            dq_part[u, :, :, :, head(n)] = jnp.transpose(dqt).astype(BF16).reshape(2, 2, shard, HD)

    def key_block(u, places):
        for n in range(heads):
            c = jnp.concatenate([col[s, b, :, pl.ds(n, 1)] for s, b in places], axis=0)
            dk_acc[n] += dot(dscores[u, n], (rows_block(qx, u, n).astype(F32) * c).astype(BF16))
            dv_acc[n] += dot(probs[u, n], (rows_block(dx, u, n).astype(F32) * c).astype(BF16))

    def p_send(s, j, tq):
        return remote(
            dq_part.at[s, j, tq],
            parts.at[t, 2 - 2 * j, s],
            p_s.at[s, j, tq],
            p_r.at[s, 1 - j, t],
            (tq, h - 1 + 2 * j, y),
        )

    def p_sib(g):
        return remote(
            dq_part.at[4 + g, :, 1 - t], parts.at[t, 1, pl.ds(2 * g, 2)], p_s.at[g, 2, 0], p_r.at[g, 2, 0], sib
        )

    def p_own(g):
        return pltpu.make_async_copy(dq_part.at[4 + g, :, t], parts.at[t, 1, pl.ds(2 * g, 2)], osem.at[4 + g])

    def give_back(s):
        combine(s)
        query_block(s, halo(s))
        both(lambda j: [p_send(s, j, tq).start() for tq in range(2)])
        for b in range(3):
            col[s, b] = jnp.transpose(row[s, b])

    def give_home(g):
        query_block(4 + g, own(g))
        p_sib(g).start()
        p_own(g).start()

    deltas(0)
    arrived(gall.at[3, first], g_s.at[4], g_r.at[4])
    arrived(gall.at[3, second], g_s.at[5], g_r.at[5])
    project_far()
    deltas(1)
    give_back(0)
    deltas(2)
    key_block(0, halo(0))
    deltas(3)
    give_back(1)
    key_block(1, halo(1))
    give_home(0)
    key_block(4, own(0))
    give_back(2)
    key_block(2, halo(2))
    give_back(3)
    give_home(1)
    key_block(5, own(1))
    key_block(3, halo(3))

    for n in range(heads):
        dv_low[:, :, head(n)] = dv_acc[n].astype(BF16).reshape(2, tile, HD)
        dk_low[:, :, head(n)] = (dk_acc[n] * SCALE).astype(BF16).reshape(2, tile, HD)
    dv_sib = remote(dv_low.at[1 - t], dv_hbm.at[:, mine], e_s.at[0], e_r.at[0], sib)
    dk_sib = remote(dk_low.at[1 - t], dk_hbm.at[:, mine], e_s.at[1], e_r.at[1], sib)
    dv_sib.start()
    dk_sib.start()
    dv_out = pltpu.make_async_copy(dv_low.at[t], dv_hbm.at[:, mine], osem.at[0])
    dk_out = pltpu.make_async_copy(dk_low.at[t], dk_hbm.at[:, mine], osem.at[1])
    dv_out.start()
    dk_out.start()

    for g in range(2):
        p_own(g).wait()
        arrived(parts.at[1 - t, 1, pl.ds(2 * g, 2)], p_s.at[g, 2, 0], p_r.at[g, 2, 0])
    for s in range(4):
        both(
            lambda d, s=s: [arrived(parts.at[c, 2 * d, s], p_s.at[s, d, c], p_r.at[s, d, c]) for c in range(2)]
        )

    @pl.when(h == 0)
    def _():
        for c in range(2):
            zero_part(0, c).wait()

    @pl.when(h == heights - 1)
    def _():
        for c in range(2):
            zero_part(2, c).wait()

    for cp in g_relays + sib_sends:
        cp.wait_send()
    both(lambda d: [q_send(c, d).wait_send() for c in range(2)])
    for i in range(4):
        both(lambda d, i=i: [d_send(i, c, d).wait_send() for c in range(2)])
        d_sib(i).wait_send()
    for s in range(4):
        both(lambda d, s=s: [p_send(s, d, tq).wait_send() for tq in range(2)])
    for g in range(2):
        p_sib(g).wait_send()
    dv_sib.wait_send()
    dk_sib.wait_send()
    arrived(dv_hbm.at[:, other], e_s.at[0], e_r.at[0])
    arrived(dk_hbm.at[:, other], e_s.at[1], e_r.at[1])
    dv_out.wait()
    dk_out.wait()


def finish(parts, dk, dv, dq_hbm, dk_hbm, dv_hbm, buf, dk_buf, dv_buf, dq_out, sem):
    y = lax.axis_index("tensor")
    shard, half = buf.shape[4:]
    loads = [
        pltpu.make_async_copy(parts.at[:, :, pl.ds(0, 2)], buf.at[0], sem.at[0]),
        pltpu.make_async_copy(parts.at[:, :, pl.ds(2, 2)], buf.at[1], sem.at[1]),
        pltpu.make_async_copy(dk, dk_buf, sem.at[2]),
        pltpu.make_async_copy(dv, dv_buf, sem.at[3]),
    ]
    stores = [
        pltpu.make_async_copy(dk_buf, dk_hbm, sem.at[4]),
        pltpu.make_async_copy(dv_buf, dv_hbm, sem.at[5]),
    ]
    for k in range(4):
        rows = pl.ds(pl.multiple_of(lax.rem(y + SHARD[k], 4) * shard, shard), shard)
        stores.append(
            pltpu.make_async_copy(
                dq_out.at[k], dq_hbm.at[rows], sem.at[6 + k]
            )
        )
    for i in (2, 3, 0, 1):
        loads[i].start()
    for i in range(2):
        loads[2 + i].wait()
        stores[i].start()
    for g in range(2):
        loads[g].wait()
        for c in range(2):
            x = buf[g, c, 0].astype(F32) + buf[g, c, 1].astype(F32) + buf[g, c, 2].astype(F32)
            dq_out[pl.ds(2 * g, 2), :, pl.ds(c * half, half)] = x.astype(BF16)
        stores[2 + 2 * g].start()
        stores[3 + 2 * g].start()
    for cp in stores:
        cp.wait()


def local(queries, key_rows, value_rows, grad_output, out_weight, window_flags, valid_counts):
    tile, width = queries.shape[3:]
    model = grad_output.shape[-1]
    half = width // 2
    heads = half // HD
    shard = tile // 4
    pair, lanes, nk = 2 * shard, 4 * shard, 2 * tile
    heights = lax.axis_size("height")
    shape = jax.ShapeDtypeStruct((tile, width), BF16)
    parts_shape = jax.ShapeDtypeStruct((2, 3, 4, shard, half), BF16)
    any_spec = pl.BlockSpec(memory_space=pl.ANY)
    dma = pltpu.SemaphoreType.DMA
    vm = pltpu.VMEM
    outs = pl.pallas_call(
        lambda *refs: kernel(heights, *refs),
        out_shape=(parts_shape, shape, shape),
        in_specs=[any_spec] * 7,
        out_specs=(any_spec, any_spec, any_spec),
        scratch_shapes=[
            vm((2, 9, 1, heights), jnp.int32),
            vm((2, 1, heights), jnp.int32),
            vm((4, shard, width), BF16),
            vm((4, shard, width), BF16),
            vm((4, shard, model), BF16),
            vm((width, model), BF16),
            vm((model, width), BF16),
            vm((6, 2, 2, shard, half), BF16),
            vm((6, 2, 2, shard, half), BF16),
            vm((2, tile, half), BF16),
            vm((2, tile, half), BF16),
            vm((heads, HD, nk), BF16),
            vm((2, nk, lanes), F32),
            vm((nk, lanes), F32),
            vm((6, heads, nk, lanes), BF16),
            vm((6, heads, nk, lanes), F32),
            vm((6, heads, nk, lanes), BF16),
            vm((heads, nk, HD), F32),
            vm((heads, nk, HD), F32),
            vm((2, tile, half), BF16),
            vm((2, tile, half), BF16),
            vm((6, 2, 2, shard, half), BF16),
            vm((4, 3, 8, pair), F32),
            vm((4, 6, 8, pair), F32),
            vm((4, 3, 8, pair), F32),
            vm((4, 3, 8, pair), F32),
            vm((4, 3, pair, 8), F32),
            dma((16,)),
            dma((6,)),
            dma((6,)),
            dma((6,)),
            dma((2, 2)),
            dma((2, 2)),
            dma((4,)),
            dma((4,)),
            dma((4, 3, 2)),
            dma((4, 3, 2)),
            dma((4, 4)),
            dma((4, 4)),
            dma((4, 3, 2)),
            dma((4, 3, 2)),
            dma((2,)),
            dma((2,)),
        ],
        compiler_params=pltpu.CompilerParams(
            collective_id=0, has_side_effects=True, vmem_limit_bytes=56 * 2**20
        ),
    )(
        window_flags.transpose(0, 3, 2, 1),
        valid_counts.transpose(0, 2, 1),
        queries.reshape(tile, width),
        key_rows.reshape(tile, width),
        value_rows.reshape(tile, width),
        grad_output.reshape(grad_output.shape[3], model),
        out_weight,
    )
    outs = pl.pallas_call(
        finish,
        out_shape=(shape, shape, shape),
        in_specs=[any_spec] * 3,
        out_specs=(any_spec,) * 3,
        scratch_shapes=[
            vm((2, 2, 3, 2, shard, half), BF16),
            vm((tile, width), BF16),
            vm((tile, width), BF16),
            vm((4, shard, width), BF16),
            dma((10,)),
        ],
    )(*outs)
    return tuple(x.reshape(queries.shape) for x in outs)


def solution(mesh):
    wide = P("tm", "height", None, None, "tensor")
    placed = (wide, wide, wide, P("tm", "height", None, "tensor", None), P("tensor", None), P(), P())
    return jax.shard_map(local, mesh=mesh, in_specs=placed, out_specs=(wide, wide, wide), check_vma=False)
```

```python
import jax
import jax.numpy as jnp
from jax import lax
from jax.experimental import pallas as pl
from jax.experimental.pallas import tpu as pltpu
from jax.sharding import PartitionSpec as P

HD = 128
SCALE = HD ** (-0.5)
LOG2E = 1.4426950408889634
MASKED = -1e30
FLOOR = -1e25
MESH = pl.DeviceIdType.MESH
F32 = jnp.float32
BF16 = jnp.bfloat16
SHARD = (0, 1, 3, 2)
NT = (((1,), (1,)), ((), ()))


def dot(a, b):
    return jnp.dot(a, b, preferred_element_type=F32)


def dot_nt(a, b):
    return lax.dot_general(a, b, NT, preferred_element_type=F32)


def kernel(
    heights,
    f_hbm,
    n_hbm,
    q_hbm,
    k_hbm,
    v_hbm,
    g_hbm,
    w_hbm,
    parts,
    dk_hbm,
    dv_hbm,
    flags,
    counts,
    qown,
    down,
    gall,
    wall,
    wt,
    qx,
    dx,
    kb,
    vb,
    kt,
    bias,
    sbuf,
    probs,
    dprobs,
    dscores,
    dk_acc,
    dv_acc,
    dk_low,
    dv_low,
    dq_part,
    st,
    rv,
    loc,
    row,
    col,
    lsem,
    osem,
    g_s,
    g_r,
    q_s,
    q_r,
    sib_s,
    sib_r,
    d_s,
    d_r,
    st_s,
    st_r,
    p_s,
    p_r,
    e_s,
    e_r,
):
    t = lax.axis_index("tm")
    h = lax.axis_index("height")
    y = lax.axis_index("tensor")
    half = k_hbm.shape[1] // 2
    heads = half // HD
    tile = k_hbm.shape[0]
    shard = tile // 4
    pair = 2 * shard
    lanes = 2 * pair
    sib = (1 - t, h, y)
    up, dn, up2, dn2 = h > 0, h < heights - 1, h > 1, h < heights - 2
    mine = pl.ds(pl.multiple_of(t * half, HD), half)
    other = pl.ds(pl.multiple_of((1 - t) * half, HD), half)

    def rows_of(k):
        return pl.ds(pl.multiple_of(lax.rem(y + SHARD[k], 4) * shard, shard), shard)

    def remote(src, dst, ssem, rsem, dev):
        return pltpu.make_async_remote_copy(
            src_ref=src, dst_ref=dst, send_sem=ssem, recv_sem=rsem, device_id=dev, device_id_type=MESH
        )

    def arrived(dst, ssem, rsem):
        remote(dst, dst, ssem, rsem, sib).wait_recv()

    def sent(src, ssem, rsem):
        remote(src, src, ssem, rsem, sib).wait_send()

    q_loads = [pltpu.make_async_copy(q_hbm.at[rows_of(k)], qown.at[k], lsem.at[k]) for k in range(4)]
    g_load = pltpu.make_async_copy(g_hbm, gall.at[0], lsem.at[4])
    k_load = pltpu.make_async_copy(k_hbm.at[:, mine], kb.at[t], lsem.at[5])
    v_load = pltpu.make_async_copy(v_hbm.at[:, mine], vb.at[t], lsem.at[6])
    w_load = pltpu.make_async_copy(w_hbm, wall, lsem.at[7])
    f_load = pltpu.make_async_copy(f_hbm, flags, lsem.at[13])
    n_load = pltpu.make_async_copy(n_hbm, counts, lsem.at[14])
    f_load.start()
    n_load.start()
    g_load.start()
    for cp in q_loads:
        cp.start()
    k_load.start()
    v_load.start()
    w_load.start()

    barrier = pltpu.get_barrier_semaphore()

    def greet(dev):
        pl.semaphore_signal(barrier, inc=1, device_id=dev, device_id_type=MESH)

    greet(sib)
    for k in (1, 2, 3):
        greet((t, h, lax.rem(y + k, 4)))

    @pl.when(up)
    def _():
        greet((0, h - 1, y))
        greet((1, h - 1, y))

    @pl.when(dn)
    def _():
        greet((0, h + 1, y))
        greet((1, h + 1, y))

    @pl.when(up2)
    def _():
        greet((t, h - 2, y))

    @pl.when(dn2)
    def _():
        greet((t, h + 2, y))

    pl.semaphore_wait(
        barrier,
        4
        + 2 * up.astype(jnp.int32)
        + 2 * dn.astype(jnp.int32)
        + up2.astype(jnp.int32)
        + dn2.astype(jnp.int32),
    )

    ahead, behind = (t, h, lax.rem(y + 1, 4)), (t, h, lax.rem(y + 3, 4))
    first, second = pl.ds(0, shard // 2), pl.ds(shard // 2, shard // 2)
    g_sends = [
        remote(g_hbm.at[first], gall.at[2, first], g_s.at[0], g_r.at[0], ahead),
        remote(g_hbm.at[second], gall.at[1, second], g_s.at[1], g_r.at[1], behind),
        remote(g_hbm.at[second], gall.at[2, second], g_s.at[2], g_r.at[2], ahead),
        remote(g_hbm.at[first], gall.at[1, first], g_s.at[3], g_r.at[3], behind),
    ]
    g_relays = [
        remote(gall.at[2, first], gall.at[3, first], g_s.at[4], g_r.at[4], ahead),
        remote(gall.at[1, second], gall.at[3, second], g_s.at[5], g_r.at[5], behind),
    ]
    for cp in g_sends:
        cp.start()
    for cp in q_loads:
        cp.wait()
    def part(c):
        return pl.ds(c * half, half)

    def q_send(p, c, d):
        return remote(
            qown.at[pl.ds(2 * p, 2), :, part(c)],
            qx.at[pl.ds(2 * p, 2), 1 - d, t],
            q_s.at[p, d, c],
            q_r.at[p, 1 - d, t],
            (c, h - 1 + 2 * d, y),
        )

    def both(fn):
        @pl.when(up)
        def _():
            fn(0)

        @pl.when(dn)
        def _():
            fn(1)

    both(lambda d: [q_send(0, c, d).start() for c in range(2)])
    sib_sends = [
        remote(k_hbm.at[:, other], kb.at[t], sib_s.at[0], sib_r.at[0], sib),
        remote(v_hbm.at[:, other], vb.at[t], sib_s.at[1], sib_r.at[1], sib),
        remote(qown.at[pl.ds(0, 2), :, other], qx.at[4, :, t], sib_s.at[2], sib_r.at[2], sib),
        remote(qown.at[pl.ds(2, 2), :, other], qx.at[5, :, t], sib_s.at[3], sib_r.at[3], sib),
    ]
    for cp in sib_sends:
        cp.start()

    q_copies = [
        pltpu.make_async_copy(qown.at[pl.ds(2 * g, 2), :, mine], qx.at[4 + g, :, t], lsem.at[(8, 15)[g]])
        for g in range(2)
    ]
    for cp in q_copies:
        cp.start()

    def zero_part(b, c):
        return pltpu.make_async_copy(dx.at[pl.ds(0, 4), b // 2, c], parts.at[c, b], osem.at[2 + c])

    def absent(b):
        for k in range(4):
            qx[k, b // 2] = jnp.zeros(qx.shape[2:], BF16)
            dx[k, b // 2] = jnp.zeros(dx.shape[2:], BF16)
        for c in range(2):
            zero_part(b, c).start()

    sub = lax.broadcasted_iota(jnp.int32, (8, pair), 0)
    nothing = jnp.where(sub < 4, FLOOR, 0.0).astype(F32)
    zeros = jnp.zeros((8, pair), F32)

    def absent_stats(i):
        for k in range(4):
            rv[k, i] = nothing

    @pl.when(h == 0)
    def _():
        absent(0)
        absent_stats(1)
        absent_stats(2)

    @pl.when(h == heights - 1)
    def _():
        absent(2)
        absent_stats(3)
        absent_stats(4)

    @pl.when(h <= 1)
    def _():
        absent_stats(0)

    @pl.when(h >= heights - 2)
    def _():
        absent_stats(5)

    for k in range(4):
        for b in range(3):
            st[k, b] = zeros
            loc[k, b] = zeros
    dk_acc[...] = jnp.zeros(dk_acc.shape, F32)
    dv_acc[...] = jnp.zeros(dv_acc.shape, F32)

    f_load.wait()
    n_load.wait()
    position = lax.broadcasted_iota(jnp.int32, (tile, pair), 0).astype(F32)
    late = lax.broadcasted_iota(jnp.int32, (1, pair), 1) >= shard
    lane = lax.broadcasted_iota(jnp.int32, (1, heights), 1)

    def at_height(values, i):
        return jnp.sum(jnp.where(lane == i, values.astype(F32), 0.0), axis=1, keepdims=True)

    for b in range(3):
        hq = h + b - 1
        inside = (hq >= 0) & (hq < heights)
        hq = jnp.clip(hq, 0, heights - 1)
        for tk in range(2):
            count = []
            for tq in range(2):
                flag = at_height(flags[tq, 3 * (tk - tq + 1) + 2 - b], hq)
                count.append(jnp.where(inside & (flag > 0.0), at_height(counts[tk], h), 0.0))
            limit = jnp.where(late, count[1], count[0])
            value = jnp.where(position < limit, 0.0, MASKED).astype(F32)
            krows = pl.ds(tk * tile, tile)
            if b == 1:
                bias[1, krows, pl.ds(0, pair)] = value
                bias[1, krows, pl.ds(pair, pair)] = value
            else:
                bias[0, krows, pl.ds((b // 2) * pair, pair)] = value

    chunk = 256
    nk = 2 * tile
    chunks = nk // chunk

    def head(n):
        return pl.ds(n * HD, HD)

    def rows_block(ref, u, n):
        return ref[u, :, :, :, head(n)].reshape(lanes, HD)

    def halo(s):
        return ((s, 0), (s, 2))

    def own(g):
        return ((2 * g, 1), (2 * g + 1, 1))

    def put(ref, places, r, value):
        for i, (s, b) in enumerate(places):
            ref[s, b, pl.ds(r, 1)] = value[:, i * pair : (i + 1) * pair]

    def score_block(u, places, which):
        for n in range(heads):
            qv = rows_block(qx, u, n)
            top = jnp.full((8, lanes), FLOOR, F32)
            for i in range(chunks):
                rows = pl.ds((i % (chunks // 2)) * chunk, chunk)
                s = dot_nt(kb[i // (chunks // 2), rows, head(n)], qv) * (SCALE * LOG2E)
                s = s + bias[which, pl.ds(i * chunk, chunk)]
                sbuf[pl.ds(i * chunk, chunk)] = s
                top = jnp.maximum(top, jnp.max(s.reshape(chunk // 8, 8, lanes), axis=0))
            m = jnp.max(top, axis=0, keepdims=True)
            total = jnp.zeros((8, lanes), F32)
            for i in range(chunks):
                e = jnp.exp2(sbuf[pl.ds(i * chunk, chunk)] - m)
                total = total + jnp.sum(e.reshape(chunk // 8, 8, lanes), axis=0)
                probs[u, n, pl.ds(i * chunk, chunk)] = e.astype(BF16)
            total = jnp.maximum(jnp.sum(total, axis=0, keepdims=True), 1e-37)
            put(loc, places, n, m)
            put(loc, places, 4 + n, 1.0 / total)
            put(st, places, n, m + jnp.log2(total))

    k_load.wait()
    v_load.wait()
    for cp in q_copies:
        cp.wait()
    arrived(kb.at[1 - t], sib_s.at[0], sib_r.at[0])
    arrived(vb.at[1 - t], sib_s.at[1], sib_r.at[1])
    arrived(qx.at[4, :, 1 - t], sib_s.at[2], sib_r.at[2])
    arrived(qx.at[5, :, 1 - t], sib_s.at[3], sib_r.at[3])
    for n in range(heads):
        kt[n] = jnp.transpose(kb[:, :, head(n)].reshape(nk, HD))
    for g in range(2):
        score_block(4 + g, own(g), 1)

    w_load.wait()
    for i in range(0, wt.shape[0], 512):
        wt[pl.ds(i, 512)] = jnp.transpose(wall[:, pl.ds(i, 512)])

    def d_send(i, c, d):
        return remote(
            down.at[i, :, part(c)],
            dx.at[i, 1 - d, t],
            d_s.at[i, d, c],
            d_r.at[i, 1 - d, t],
            (c, h - 1 + 2 * d, y),
        )

    def d_sib(i):
        return remote(
            down.at[i, :, other], dx.at[4 + i // 2, i % 2, t], d_s.at[i, 2, 0], d_r.at[i, 2, 0], sib
        )

    def d_own(i):
        return pltpu.make_async_copy(down.at[i, :, mine], dx.at[4 + i // 2, i % 2, t], lsem.at[9 + i])

    def project(i, count):
        src = gall[pl.ds(i, count)].reshape(count * shard, gall.shape[2])
        d = dot(src, wt[...]).astype(BF16)
        down[pl.ds(i, count)] = d.reshape(count, shard, d.shape[1])

    def d_go(i):
        both(lambda d: [d_send(i, c, d).start() for c in range(2)])
        d_sib(i).start()
        d_own(i).start()

    def project_far():
        for c in range(2):
            down[3, :, part(c)] = dot(gall[3], wt[:, part(c)]).astype(BF16)
            both(lambda d, c=c: d_send(3, c, d).start())
        d_sib(3).start()
        d_own(3).start()

    def d_here(i):
        d_own(i).wait()
        arrived(dx.at[4 + i // 2, i % 2, 1 - t], d_s.at[i, 2, 0], d_r.at[i, 2, 0])

    def d_near(i):
        both(
            lambda d: [arrived(dx.at[i, d, tq], d_s.at[i, d, tq], d_r.at[i, d, tq]) for tq in range(2)]
        )

    g_load.wait()
    project(0, 1)
    d_go(0)
    both(lambda d: [q_send(1, c, d).start() for c in range(2)])

    def halo_scores(p):
        both(
            lambda d: [
                arrived(qx.at[pl.ds(2 * p, 2), d, tq], q_s.at[p, d, tq], q_r.at[p, d, tq]) for tq in range(2)
            ]
        )

        @pl.loop(2 * p, 2 * p + 2)
        def _(s):
            score_block(s, halo(s), 0)

    halo_scores(0)
    arrived(gall.at[2, first], g_s.at[0], g_r.at[0])
    arrived(gall.at[1, second], g_s.at[1], g_r.at[1])
    for cp in g_sends:
        cp.wait_send()
    for cp in g_relays:
        cp.start()
    arrived(gall.at[1, first], g_s.at[3], g_r.at[3])
    arrived(gall.at[2, second], g_s.at[2], g_r.at[2])
    project(1, 2)
    d_go(1)
    d_go(2)

    def exchange(own, got, ssem, rsem):
        def copies():
            return (
                (up, remote(own.at[pl.ds(0, 2)], got.at[pl.ds(3, 2)], ssem.at[0], rsem.at[1], (t, h - 1, y))),
                (dn, remote(own.at[pl.ds(1, 2)], got.at[pl.ds(1, 2)], ssem.at[1], rsem.at[0], (t, h + 1, y))),
                (up2, remote(own.at[0], got.at[5], ssem.at[2], rsem.at[3], (t, h - 2, y))),
                (dn2, remote(own.at[2], got.at[0], ssem.at[3], rsem.at[2], (t, h + 2, y))),
            )

        def go():
            for cond, cp in copies():
                pl.when(cond)(cp.start)

        def finish():
            for cond, cp in copies():
                pl.when(cond)(cp.wait_send)
            for cond, dst, i in (
                (up, got.at[pl.ds(1, 2)], 0),
                (dn, got.at[pl.ds(3, 2)], 1),
                (up2, got.at[0], 2),
                (dn2, got.at[5], 3),
            ):
                pl.when(cond)(lambda dst=dst, i=i: arrived(dst, ssem.at[i], rsem.at[i]))

        return go, finish

    swaps = [exchange(st.at[s], rv.at[s], st_s.at[s], st_r.at[s]) for s in range(4)]

    def delta_block(u, s, places, cols):
        size = cols.size
        for n in range(heads):
            if size == lanes:
                d = rows_block(dx, u, n)
            else:
                d = dx[u, s % 2, :, :, head(n)].reshape(pair, HD)
            total = jnp.zeros((8, size), F32)
            for i in range(chunks):
                rows = pl.ds((i % (chunks // 2)) * chunk, chunk)
                dp = dot_nt(vb[i // (chunks // 2), rows, head(n)], d)
                krows = pl.ds(i * chunk, chunk)
                dprobs[u, n, krows, cols] = dp
                x = dp * probs[u, n, krows, cols].astype(F32)
                total = total + jnp.sum(x.reshape(chunk // 8, 8, size), axis=0)
            total = jnp.sum(total, axis=0, keepdims=True)
            scale = [loc[k, b, pl.ds(4 + n, 1)] for k, b in places]
            scale = scale[0] if len(scale) == 1 else jnp.concatenate(scale, axis=1)
            put(st, places, 4 + n, total * scale)

    def deltas(s):
        d_here(s)
        delta_block(4 + s // 2, s, ((s, 1),), pl.ds((s % 2) * pair, pair))
        d_near(s)
        delta_block(s, s, halo(s), pl.ds(0, lanes))
        swaps[s][0]()

    def combine(s):
        swaps[s][1]()
        for b in range(3):
            x = [st[s, b], rv[s, 2 * b], rv[s, 2 * b + 1]]
            lse = [v[0:4] for v in x]
            top = jnp.maximum(jnp.maximum(lse[0], lse[1]), lse[2])
            weight = [jnp.exp2(v - top) for v in lse]
            total = weight[0] + weight[1] + weight[2]
            delta = (weight[0] * x[0][4:8] + weight[1] * x[1][4:8] + weight[2] * x[2][4:8]) / total
            c = jnp.exp2(loc[s, b, pl.ds(0, 4)] - (top + jnp.log2(total)))
            row[s, b] = jnp.concatenate([c, delta], axis=0)

    def query_block(u, places):
        for n in range(heads):
            c, delta = [
                jnp.concatenate([row[s, b, pl.ds(r, 1)] for s, b in places], axis=1) for r in (n, 4 + n)
            ]
            ds = (probs[u, n].astype(F32) * (dprobs[u, n] - delta)).astype(BF16)
            dscores[u, n] = ds
            dqt = dot(kt[n], ds) * (c * SCALE)
            dq_part[u, :, :, :, head(n)] = jnp.transpose(dqt).astype(BF16).reshape(2, 2, shard, HD)

    def key_block(u, places):
        for n in range(heads):
            c = jnp.concatenate([col[s, b, :, pl.ds(n, 1)] for s, b in places], axis=0)
            dk_acc[n] += dot(dscores[u, n], (rows_block(qx, u, n).astype(F32) * c).astype(BF16))
            dv_acc[n] += dot(probs[u, n], (rows_block(dx, u, n).astype(F32) * c).astype(BF16))

    def p_send(s, j, tq):
        return remote(
            dq_part.at[s, j, tq],
            parts.at[t, 2 - 2 * j, s],
            p_s.at[s, j, tq],
            p_r.at[s, 1 - j, t],
            (tq, h - 1 + 2 * j, y),
        )

    def p_sib(g):
        return remote(
            dq_part.at[4 + g, :, 1 - t], parts.at[t, 1, pl.ds(2 * g, 2)], p_s.at[g, 2, 0], p_r.at[g, 2, 0], sib
        )

    def p_own(g):
        return pltpu.make_async_copy(dq_part.at[4 + g, :, t], parts.at[t, 1, pl.ds(2 * g, 2)], osem.at[4 + g])

    def give_back(s):
        combine(s)
        query_block(s, halo(s))
        both(lambda j: [p_send(s, j, tq).start() for tq in range(2)])
        for b in range(3):
            col[s, b] = jnp.transpose(row[s, b])

    def give_home(g):
        query_block(4 + g, own(g))
        p_sib(g).start()
        p_own(g).start()

    deltas(0)
    halo_scores(1)
    arrived(gall.at[3, first], g_s.at[4], g_r.at[4])
    arrived(gall.at[3, second], g_s.at[5], g_r.at[5])
    project_far()
    deltas(1)
    give_back(0)
    deltas(2)
    key_block(0, halo(0))
    deltas(3)
    give_back(1)
    key_block(1, halo(1))
    give_home(0)
    key_block(4, own(0))
    give_back(2)
    key_block(2, halo(2))
    give_back(3)
    give_home(1)
    key_block(5, own(1))
    key_block(3, halo(3))

    for n in range(heads):
        dv_low[:, :, head(n)] = dv_acc[n].astype(BF16).reshape(2, tile, HD)
        dk_low[:, :, head(n)] = (dk_acc[n] * SCALE).astype(BF16).reshape(2, tile, HD)
    dv_sib = remote(dv_low.at[1 - t], dv_hbm.at[:, mine], e_s.at[0], e_r.at[0], sib)
    dk_sib = remote(dk_low.at[1 - t], dk_hbm.at[:, mine], e_s.at[1], e_r.at[1], sib)
    dv_sib.start()
    dk_sib.start()
    dv_out = pltpu.make_async_copy(dv_low.at[t], dv_hbm.at[:, mine], osem.at[0])
    dk_out = pltpu.make_async_copy(dk_low.at[t], dk_hbm.at[:, mine], osem.at[1])
    dv_out.start()
    dk_out.start()

    for g in range(2):
        p_own(g).wait()
        arrived(parts.at[1 - t, 1, pl.ds(2 * g, 2)], p_s.at[g, 2, 0], p_r.at[g, 2, 0])
    for s in range(4):
        both(
            lambda d, s=s: [arrived(parts.at[c, 2 * d, s], p_s.at[s, d, c], p_r.at[s, d, c]) for c in range(2)]
        )

    @pl.when(h == 0)
    def _():
        for c in range(2):
            zero_part(0, c).wait()

    @pl.when(h == heights - 1)
    def _():
        for c in range(2):
            zero_part(2, c).wait()

    for cp in g_relays + sib_sends:
        cp.wait_send()
    for p in range(2):
        both(lambda d, p=p: [q_send(p, c, d).wait_send() for c in range(2)])
    for i in range(4):
        both(lambda d, i=i: [d_send(i, c, d).wait_send() for c in range(2)])
        d_sib(i).wait_send()
    for s in range(4):
        both(lambda d, s=s: [p_send(s, d, tq).wait_send() for tq in range(2)])
    for g in range(2):
        p_sib(g).wait_send()
    dv_sib.wait_send()
    dk_sib.wait_send()
    arrived(dv_hbm.at[:, other], e_s.at[0], e_r.at[0])
    arrived(dk_hbm.at[:, other], e_s.at[1], e_r.at[1])
    dv_out.wait()
    dk_out.wait()


def finish(parts, dk, dv, dq_hbm, dk_hbm, dv_hbm, buf, dk_buf, dv_buf, dq_out, sem):
    y = lax.axis_index("tensor")
    shard, half = buf.shape[4:]
    loads = [
        pltpu.make_async_copy(parts.at[:, :, pl.ds(0, 2)], buf.at[0], sem.at[0]),
        pltpu.make_async_copy(parts.at[:, :, pl.ds(2, 2)], buf.at[1], sem.at[1]),
        pltpu.make_async_copy(dk, dk_buf, sem.at[2]),
        pltpu.make_async_copy(dv, dv_buf, sem.at[3]),
    ]
    stores = [
        pltpu.make_async_copy(dk_buf, dk_hbm, sem.at[4]),
        pltpu.make_async_copy(dv_buf, dv_hbm, sem.at[5]),
    ]
    for k in range(4):
        rows = pl.ds(pl.multiple_of(lax.rem(y + SHARD[k], 4) * shard, shard), shard)
        stores.append(
            pltpu.make_async_copy(
                dq_out.at[k], dq_hbm.at[rows], sem.at[6 + k]
            )
        )
    for i in (2, 3, 0, 1):
        loads[i].start()
    for i in range(2):
        loads[2 + i].wait()
        stores[i].start()
    for g in range(2):
        loads[g].wait()
        for c in range(2):
            x = buf[g, c, 0].astype(F32) + buf[g, c, 1].astype(F32) + buf[g, c, 2].astype(F32)
            dq_out[pl.ds(2 * g, 2), :, pl.ds(c * half, half)] = x.astype(BF16)
        stores[2 + 2 * g].start()
        stores[3 + 2 * g].start()
    for cp in stores:
        cp.wait()


def local(queries, key_rows, value_rows, grad_output, out_weight, window_flags, valid_counts):
    tile, width = queries.shape[3:]
    model = grad_output.shape[-1]
    half = width // 2
    heads = half // HD
    shard = tile // 4
    pair, lanes, nk = 2 * shard, 4 * shard, 2 * tile
    heights = lax.axis_size("height")
    shape = jax.ShapeDtypeStruct((tile, width), BF16)
    parts_shape = jax.ShapeDtypeStruct((2, 3, 4, shard, half), BF16)
    any_spec = pl.BlockSpec(memory_space=pl.ANY)
    dma = pltpu.SemaphoreType.DMA
    vm = pltpu.VMEM
    outs = pl.pallas_call(
        lambda *refs: kernel(heights, *refs),
        out_shape=(parts_shape, shape, shape),
        in_specs=[any_spec] * 7,
        out_specs=(any_spec, any_spec, any_spec),
        scratch_shapes=[
            vm((2, 9, 1, heights), jnp.int32),
            vm((2, 1, heights), jnp.int32),
            vm((4, shard, width), BF16),
            vm((4, shard, width), BF16),
            vm((4, shard, model), BF16),
            vm((width, model), BF16),
            vm((model, width), BF16),
            vm((6, 2, 2, shard, half), BF16),
            vm((6, 2, 2, shard, half), BF16),
            vm((2, tile, half), BF16),
            vm((2, tile, half), BF16),
            vm((heads, HD, nk), BF16),
            vm((2, nk, lanes), F32),
            vm((nk, lanes), F32),
            vm((6, heads, nk, lanes), BF16),
            vm((6, heads, nk, lanes), F32),
            vm((6, heads, nk, lanes), BF16),
            vm((heads, nk, HD), F32),
            vm((heads, nk, HD), F32),
            vm((2, tile, half), BF16),
            vm((2, tile, half), BF16),
            vm((6, 2, 2, shard, half), BF16),
            vm((4, 3, 8, pair), F32),
            vm((4, 6, 8, pair), F32),
            vm((4, 3, 8, pair), F32),
            vm((4, 3, 8, pair), F32),
            vm((4, 3, pair, 8), F32),
            dma((16,)),
            dma((6,)),
            dma((6,)),
            dma((6,)),
            dma((2, 2, 2)),
            dma((2, 2, 2)),
            dma((4,)),
            dma((4,)),
            dma((4, 3, 2)),
            dma((4, 3, 2)),
            dma((4, 4)),
            dma((4, 4)),
            dma((4, 3, 2)),
            dma((4, 3, 2)),
            dma((2,)),
            dma((2,)),
        ],
        compiler_params=pltpu.CompilerParams(
            collective_id=0, has_side_effects=True, vmem_limit_bytes=56 * 2**20
        ),
    )(
        window_flags.transpose(0, 3, 2, 1),
        valid_counts.transpose(0, 2, 1),
        queries.reshape(tile, width),
        key_rows.reshape(tile, width),
        value_rows.reshape(tile, width),
        grad_output.reshape(grad_output.shape[3], model),
        out_weight,
    )
    outs = pl.pallas_call(
        finish,
        out_shape=(shape, shape, shape),
        in_specs=[any_spec] * 3,
        out_specs=(any_spec,) * 3,
        scratch_shapes=[
            vm((2, 2, 3, 2, shard, half), BF16),
            vm((tile, width), BF16),
            vm((tile, width), BF16),
            vm((4, shard, width), BF16),
            dma((10,)),
        ],
    )(*outs)
    return tuple(x.reshape(queries.shape) for x in outs)


def solution(mesh):
    wide = P("tm", "height", None, None, "tensor")
    placed = (wide, wide, wide, P("tm", "height", None, "tensor", None), P("tensor", None), P(), P())
    return jax.shard_map(local, mesh=mesh, in_specs=placed, out_specs=(wide, wide, wide), check_vma=False)
```
